32 devices in a mesh: groups: 2 (over y), rows: 8 (over z, x), heads: 2 (over core).
Axes of the slice: x: 2, y: 2, z: 4, core: 2. Of those that a mesh axis runs over, the one named last changes fastest.
Arguments:
- residual_in: bfloat16 [128, 8192], P(('groups', 'rows'), 'heads'), parts along dimension 0, may hold values from -6 to 6
- query: bfloat16 [128, 8192], P(('groups', 'rows'), 'heads'), parts along dimension 0, may hold values from -120 to 120
- key_cache: bfloat16 [128, 4, 32, 128], P(('groups', 'rows'), 'heads'), parts along dimension 0, may hold values from -4 to 4
- value_cache: bfloat16 [128, 4, 32, 128], P(('groups', 'rows'), 'heads'), parts along dimension 0, may hold values from -5 to 5
- key_new: bfloat16 [128, 4, 128], P(('groups', 'rows'), 'heads'), parts along dimension 0, may hold values from -4 to 4
- value_new: bfloat16 [128, 4, 128], P(('groups', 'rows'), 'heads'), parts along dimension 0, may hold values from -5 to 5
- lengths: int32 [128], P(('groups', 'rows')), parts along dimension 0, may hold values from 2 to 32, as said below
- norm_gain: bfloat16 [8192], replicated, may hold values from 0.3984375 to 1.59375
- hot_gate: bfloat16 [128, 8192], P('heads'), may hold values from -0.0625 to 0.0625
- hot_up: bfloat16 [128, 8192], P('heads'), may hold values from -0.0625 to 0.0625
- hot_down: bfloat16 [128, 8192], P('heads'), may hold values from -0.5 to 0.5
- cold_gate: bfloat16 [512, 8192], P(('rows', 'heads')), may hold values from -0.0625 to 0.0625
- cold_up: bfloat16 [512, 8192], P(('rows', 'heads')), may hold values from -0.0625 to 0.0625
- cold_down: bfloat16 [512, 8192], P(('rows', 'heads')), may hold values from -0.5 to 0.5
- active: int32 [128, 4], P(('groups', 'rows')), parts along dimension 0, may hold values from 0 to 1, as said below
Outputs:
- residual_out: bfloat16 [128, 8192], P(('groups', 'rows'), 'heads'), parts along dimension 0
The draws below stay inside these ranges and needn't reach their ends.
There are 2 independent parts, one for each index of `groups`. The reference program is written for one: setup_inputs(seed, part) draws one part's arguments, and reference() takes and returns one part's arrays. A program takes and returns all parts, laid end to end along the dimension named above; an argument that names none is the same for every part. Nothing has to cross between parts.
Inputs may be any that keep to these rules, and one draw needn't show every extreme that they name: `lengths`: every request has at least two filled slots, and some request has all 32. `active`: 0 or 1; among the 8 requests of one index of rows at most 2 are active on any one cold block, and exactly 2 on some.
All inputs are finite; a program needn't handle non-finite values.
Results may differ from the reference program's by a relative error of at most 0.0085.
Values may be sent and summed in bfloat16 or wider, within the bound.
A program may use at most 64 MiB of HBM per device.

```python
import jax
import jax.numpy as jnp
from jax import lax

HD = 128
QH = 64
KVH = 4
D = 8192
GROUP = 16
BLOCK = 128
HOT = 1
CAP = 2
REQ_DEV = 8
CTX = 32
REQS = 64
NCOLD = 4


def shared_pair(key):
    keys_all = jnp.clip(jax.random.normal(jax.random.fold_in(key, 11), (REQS, KVH, CTX, HD), jnp.float32), -4.0, 4.0)
    queries = jnp.clip(jax.random.normal(jax.random.fold_in(key, 12), (REQS, QH, HD), jnp.float32), -4.0, 4.0)
    return (queries.reshape(REQS, QH * HD), keys_all)


def draw_query(key, part):
    return shared_pair(key)[0].astype(jnp.bfloat16)


def draw_key_cache(key, part):
    return shared_pair(key)[1].astype(jnp.bfloat16)


def draw_lengths(key, part):
    drawn = jax.random.randint(jax.random.fold_in(key, 21), (REQS,), 2, CTX + 1)
    return drawn.at[0].set(CTX).astype(jnp.int32)


def draw_active(key, part):
    owners = REQS // REQ_DEV
    levels = jax.random.randint(jax.random.fold_in(key, 32), (NCOLD,), 1, 7)
    rolled = jax.random.randint(jax.random.fold_in(key, 31), (REQS, NCOLD), 0, 16)
    switched = (rolled < levels[None, :]).astype(jnp.int32)
    switched = switched.at[0:CAP, 0].set(1)
    grouped = switched.reshape(owners, REQ_DEV, NCOLD)
    before = jnp.cumsum(grouped, axis=1) - grouped
    kept = grouped * (before < CAP).astype(jnp.int32)
    return kept.reshape(REQS, NCOLD).astype(jnp.int32)


def block_scale(key, dims, split, low, top_value):
    factor_of, own = 1.0, jax.random.fold_in(key, 6)
    for position, blocks in split:
        draws = jnp.exp(jax.random.uniform(jax.random.fold_in(own, position), (blocks,), jnp.float32, low / len(split), top_value / len(split)))
        factor_of = factor_of * jnp.repeat(draws, dims[position] // blocks).reshape([-1 if axis == position else 1 for axis in range(len(dims))])
    return factor_of


def bell_draw(own_key, extent, scale, most, split=(), held_as=jnp.bfloat16):
    factor_of = block_scale(own_key, extent, split, -0.22, 0.18) if split else 1.0
    array = jax.random.normal(own_key, extent, jnp.float32) * scale * factor_of
    return jnp.minimum(jnp.maximum(array, -most), most).astype(held_as)


def setup_inputs(seed: int = 0, part: int = 0) -> dict:
    keys = jax.random.split(jax.random.key(seed), 16)
    part_keys = jax.random.split(jax.random.fold_in(keys[15], part), 16)
    residual_in = bell_draw(part_keys[0], (REQS, D), 1.0, 6.0, ((0, 8), (1, 2)))
    query = draw_query(jax.random.fold_in(jax.random.fold_in(keys[15], part), 71), part)
    key_cache = draw_key_cache(jax.random.fold_in(jax.random.fold_in(keys[15], part), 71), part)
    value_cache = bell_draw(part_keys[3], (REQS, KVH, CTX, HD), 1.0, 5.0, ((0, 8), (1, 2)))
    key_new = bell_draw(part_keys[4], (REQS, KVH, HD), 1.0, 4.0, ((0, 8), (1, 2)))
    value_new = bell_draw(part_keys[5], (REQS, KVH, HD), 1.0, 5.0, ((0, 8), (1, 2)))
    lengths = draw_lengths(jax.random.fold_in(jax.random.fold_in(keys[15], part), 71), part)
    norm_gain = jnp.clip(1.0 + 0.12 * jax.random.normal(keys[7], (D,), jnp.float32), 0.3984375, 1.59375).astype(jnp.bfloat16)
    hot_gate = bell_draw(keys[8], (HOT * BLOCK, D), D ** -0.5, 0.0625, ((0, 2),))
    hot_up = bell_draw(keys[9], (HOT * BLOCK, D), D ** -0.5, 0.0625, ((0, 2),))
    hot_down = bell_draw(keys[10], (HOT * BLOCK, D), BLOCK ** -0.5, 0.5, ((0, 2),))
    cold_gate = bell_draw(keys[11], (NCOLD * BLOCK, D), D ** -0.5, 0.0625, ((0, 16),))
    cold_up = bell_draw(keys[12], (NCOLD * BLOCK, D), D ** -0.5, 0.0625, ((0, 16),))
    cold_down = bell_draw(keys[13], (NCOLD * BLOCK, D), BLOCK ** -0.5, 0.5, ((0, 16),))
    active = draw_active(jax.random.fold_in(jax.random.fold_in(keys[15], part), 71), part)
    return {"residual_in": residual_in, "query": query, "key_cache": key_cache, "value_cache": value_cache, "key_new": key_new, "value_new": value_new, "lengths": lengths, "norm_gain": norm_gain, "hot_gate": hot_gate, "hot_up": hot_up, "hot_down": hot_down, "cold_gate": cold_gate, "cold_up": cold_up, "cold_down": cold_down, "active": active}


def attention_rows(query, key_cache, value_cache, key_new, value_new, lengths):
    count = query.shape[0]
    scale_factor = 1.0 / HD ** 0.5
    queries = query.astype(jnp.float32).reshape(count, KVH, GROUP, HD)
    scores = jnp.einsum('rgjd,rgpd->rgjp', queries, key_cache.astype(jnp.float32)) * scale_factor
    own_score = jnp.einsum('rgjd,rgd->rgj', queries, key_new.astype(jnp.float32)) * scale_factor
    visible = (jnp.arange(CTX, dtype=jnp.int32)[None, :] < lengths[:, None])[:, None, None, :]
    scores = jnp.where(visible, scores, -1e+30)
    highest = jnp.maximum(lax.optimization_barrier(jnp.max(scores, axis=-1)), own_score)
    expons = jnp.where(visible, jnp.exp(scores - highest[..., None]), 0.0)
    own_expon = jnp.exp(own_score - highest)
    totals = lax.optimization_barrier(jnp.sum(expons, axis=-1)) + own_expon
    weights = (expons / totals[..., None]).astype(jnp.bfloat16)
    own_weight = (own_expon / totals).astype(jnp.bfloat16)
    blended = jnp.einsum('rgjp,rgpd->rgjd', weights.astype(jnp.float32), value_cache.astype(jnp.float32))
    blended = blended + own_weight.astype(jnp.float32)[..., None] * value_new.astype(jnp.float32)[:, :, None, :]
    return blended.reshape(count, QH * HD)

def swiglu(normed, gate_rows, up_rows):
    gate = jnp.dot(normed, gate_rows.T, preferred_element_type=jnp.float32)
    upper = jnp.dot(normed, up_rows.T, preferred_element_type=jnp.float32)
    return jax.nn.silu(gate) * upper

def reference(residual_in, query, key_cache, value_cache, key_new, value_new, lengths, norm_gain, hot_gate, hot_up, hot_down, cold_gate, cold_up, cold_down, active):
    attended = attention_rows(query, key_cache, value_cache, key_new, value_new, lengths)
    stream = (residual_in.astype(jnp.float32) + attended).astype(jnp.bfloat16)
    wide = stream.astype(jnp.float32)
    mean_sq = lax.optimization_barrier(jnp.mean(wide * wide, axis=-1, keepdims=True))
    normed = (wide * jax.lax.rsqrt(mean_sq + 1e-05) * norm_gain.astype(jnp.float32)).astype(jnp.bfloat16)
    hot_hidden = swiglu(normed, hot_gate, hot_up).astype(jnp.bfloat16)
    hot_part = jnp.dot(hot_hidden, hot_down, preferred_element_type=jnp.float32)
    neuron_mask = jnp.repeat(active.astype(jnp.float32), BLOCK, axis=1)
    cold_hidden = (swiglu(normed, cold_gate, cold_up) * neuron_mask).astype(jnp.bfloat16)
    cold_part = jnp.dot(cold_hidden, cold_down, preferred_element_type=jnp.float32)
    return (stream.astype(jnp.float32) + hot_part + cold_part).astype(jnp.bfloat16)
```

```python
import functools

import jax
import jax.numpy as jnp
from jax import lax
from jax.experimental import pallas as pl
from jax.experimental.pallas import tpu as pltpu
from jax.sharding import PartitionSpec as P

HD = 128
GROUP = 16
CAP = 2
REQ = 8
LANES = 512
F32 = jnp.float32
BF16 = jnp.bfloat16
MESH = pl.DeviceIdType.MESH


def iota(shape, axis):
    return lax.broadcasted_iota(jnp.int32, shape, axis)


def onehot(hit):
    return jnp.where(hit, 1.0, 0.0).astype(BF16)


def dot(a, b):
    return jnp.dot(a, b, preferred_element_type=F32)


def dot_t(a, b):
    return lax.dot_general(a, b, (((1,), (1,)), ((), ())), preferred_element_type=F32)


def loop(count, body):
    if count <= 8:
        for step in range(count):
            body(step)
    else:
        lax.fori_loop(0, count, lambda step, carry: (body(step), carry)[1], 0)


def kernel(n, nb, ctx, nhot, ncold, width, *refs):
    (
        q_ref, res_ref, kn_ref, vn_ref, gain_ref, len_ref, act_ref,
        kc_hbm, vc_hbm, hg_hbm, hu_hbm, hd_hbm, cg_hbm, cu_hbm, cd_hbm,
        out_ref,
        kc_v, vc_v, hgu_v, hd_v, cgu_v, cd_v,
        xh, dsp, inc, rout, ret, hot_send, hot_recv, cold_acc,
        load_sem, swap_send, swap_recv, x_sem, hot_sem,
        dsp_sem, inc_sem, rout_sem, ret_sem,
    ) = refs
    half = width // 2
    chunks = half // LANES
    per = n // nb
    row = lax.axis_index("rows")
    h = lax.axis_index("heads")
    other = 1 - h
    t = lax.rem(row, 2)
    idx = lax.div(row, 2)
    partner = {"heads": other}

    loads = [
        (kc_hbm, kc_v),
        (vc_hbm, vc_v),
        (cg_hbm, cgu_v.at[pl.ds(pl.multiple_of(h * ncold, ncold), ncold)]),
        (cu_hbm, cgu_v.at[pl.ds(pl.multiple_of((2 + h) * ncold, ncold), ncold)]),
        (hg_hbm, hgu_v.at[pl.ds(0, nhot)]),
        (hu_hbm, hgu_v.at[pl.ds(nhot, nhot)]),
        (cd_hbm, cd_v.at[pl.ds(pl.multiple_of(h * ncold, ncold), ncold)]),
        (hd_hbm, hd_v),
    ]
    loads = [
        pltpu.make_async_copy(src, dst, load_sem.at[i]) for i, (src, dst) in enumerate(loads)
    ]
    for copy in loads:
        copy.start()

    barrier = pltpu.get_barrier_semaphore()

    def greet(step):
        peer = lax.rem(row + step, n)
        for side in range(2):
            @pl.when(jnp.logical_or(peer != row, h != side))
            def _():
                pl.semaphore_signal(
                    barrier, inc=1, device_id={"rows": peer, "heads": side}, device_id_type=MESH
                )

    loop(n, greet)

    scale = 1.0 / HD**0.5
    span = REQ * ctx
    rows_q = GROUP * REQ
    col = iota((rows_q, span), 1)
    filled = jnp.zeros((rows_q, span), jnp.int32)
    for r in range(REQ):
        filled = jnp.where(lax.div(col, ctx) == r, len_ref[r], filled)
    mask = jnp.logical_and(
        lax.rem(iota((rows_q, span), 0), REQ) == lax.div(col, ctx), lax.rem(col, ctx) < filled
    )
    q = q_ref[...].astype(F32)
    residual = res_ref[...].astype(F32)
    kv_local = kc_v.shape[1]
    tiles = []

    def attend(g):
        qs = jnp.concatenate(
            [q[:, (g * GROUP + j) * HD:(g * GROUP + j + 1) * HD] for j in range(GROUP)], axis=0
        )
        keys = kc_v[:, g].reshape(span, HD)
        s = dot_t(qs.astype(BF16), keys) * scale
        key_own = jnp.concatenate([kn_ref[:, g, :].astype(F32)] * GROUP, axis=0)
        own = jnp.sum(qs * key_own, axis=-1, keepdims=True) * scale
        s = jnp.where(mask, s, -1e30)
        top = jnp.maximum(jnp.max(s, axis=-1, keepdims=True), own)
        e = jnp.where(mask, jnp.exp(s - top), 0.0)
        e_own = jnp.exp(own - top)
        inv = 1.0 / (jnp.sum(e, axis=-1, keepdims=True) + e_own)
        w = (e * inv).astype(BF16)
        w_own = (e_own * inv).astype(BF16).astype(F32)
        value_own = jnp.concatenate([vn_ref[:, g, :].astype(F32)] * GROUP, axis=0)
        o = dot(w, vc_v[:, g].reshape(span, HD)) + w_own * value_own
        for j in range(GROUP):
            tiles.append(o[j * REQ:(j + 1) * REQ])

    loads[0].wait()
    loads[1].wait()
    attend(0)

    pl.semaphore_wait(barrier, 2 * n - 1)
    swaps = [
        (cg_hbm, cgu_v.at[pl.ds(pl.multiple_of(h * ncold, ncold), ncold)]),
        (cu_hbm, cgu_v.at[pl.ds(pl.multiple_of((2 + h) * ncold, ncold), ncold)]),
        (cd_hbm, cd_v.at[pl.ds(pl.multiple_of(h * ncold, ncold), ncold)]),
    ]
    swaps = [
        pltpu.make_async_remote_copy(
            src, dst, swap_send.at[i], swap_recv.at[i], device_id=partner, device_id_type=MESH
        )
        for i, (src, dst) in enumerate(swaps)
    ]
    for copy in swaps:
        copy.start()

    for g in range(1, kv_local):
        attend(g)

    per_chunk = LANES // HD
    x = jnp.concatenate(
        [
            residual[:, c * LANES:(c + 1) * LANES]
            + jnp.concatenate(tiles[c * per_chunk:(c + 1) * per_chunk], axis=1)
            for c in range(chunks)
        ],
        axis=0,
    ).astype(BF16)
    xh[h] = x

    def slots(first):
        found = []
        for b in range(4):
            count = jnp.int32(0)
            places = [jnp.int32(-1)] * CAP
            for r in range(REQ):
                on = act_ref[r, first + b]
                for s in range(CAP):
                    places[s] = jnp.where(
                        jnp.logical_and(on == 1, count == s), jnp.int32(r), places[s]
                    )
                count = count + on
            found += places
        return found

    stack = chunks * REQ
    pay = CAP * chunks

    def select(i):
        shape = (4 * pay, stack)
        line = iota(shape, 0)
        place = jnp.full(shape, -1, jnp.int32)
        for k, p in enumerate(slots(i * 4)):
            place = jnp.where(lax.div(line, chunks) == k, p, place)
        other_col = iota(shape, 1)
        hit = jnp.logical_and(
            lax.rem(line, chunks) == lax.div(other_col, REQ), lax.rem(other_col, REQ) == place
        )
        dsp[pl.ds(i * 4, 4)] = dot(onehot(hit), x).astype(BF16).reshape(4, pay, LANES)

    loop(nb // 4, select)

    def dispatch(step):
        dst = lax.rem(row + step, n)
        return pltpu.make_async_remote_copy(
            dsp.at[lax.div(dst, per)], inc.at[idx, h], dsp_sem.at[step], inc_sem.at[idx, h],
            device_id={"rows": dst, "heads": t}, device_id_type=MESH,
        )

    dispatch_own = pltpu.make_async_copy(
        dsp.at[lax.div(row, per)], inc.at[idx, h], inc_sem.at[idx, h]
    )
    loop(n - 1, lambda step: dispatch(step + 1).start())

    @pl.when(t == h)
    def _():
        dispatch_own.start()

    @pl.when(t != h)
    def _():
        dispatch(0).start()

    send_x = pltpu.make_async_remote_copy(
        xh.at[h], xh.at[h], x_sem.at[0], x_sem.at[1], device_id=partner, device_id_type=MESH
    )
    send_x.start()

    def hidden(blocks, weights, count):
        total = blocks[0] * blocks[0]
        for block in blocks[1:]:
            total = total + block * block
        rs = lax.rsqrt(jnp.sum(total, axis=-1, keepdims=True) / width + 1e-05)
        normed = jnp.concatenate(
            [
                (
                    block * rs * gain_ref[:, c * LANES:(c + 1) * LANES].astype(F32)
                ).astype(BF16)
                for c, block in enumerate(blocks)
            ],
            axis=1,
        )
        both = dot_t(normed, weights)
        gate, up = both[:, :count], both[:, count:]
        return (gate / (1.0 + jnp.exp(-gate)) * up).astype(BF16)

    loads[4].wait()
    loads[5].wait()
    send_x.wait()
    whole = [xh[side].astype(F32) for side in range(2)]
    hot_hidden = hidden(
        [whole[c // chunks][(c % chunks) * REQ:(c % chunks + 1) * REQ] for c in range(2 * chunks)],
        hgu_v[...],
        nhot,
    )

    loads[2].wait()
    loads[3].wait()
    loads[6].wait()
    for copy in swaps:
        copy.wait()

    big = 4 * 2 * pay
    a, b = iota((big, big), 0), iota((big, big), 1)

    def packed(v):
        hf, c = lax.div(v, chunks * 8), lax.rem(lax.div(v, 8), chunks)
        i, s = lax.rem(lax.div(v, 2), 4), lax.rem(v, 2)
        return ((i * 2 + hf) * CAP + s) * chunks + c

    gather = onehot(packed(a) == b)
    scatter = onehot(packed(b) == a)

    def returns(i, hf):
        dst = 2 * i + h
        return (
            jnp.logical_and(dst == row, hf == h),
            pltpu.make_async_remote_copy(
                rout.at[i, hf], ret.at[row], rout_sem.at[i, hf], ret_sem.at[row],
                device_id={"rows": dst, "heads": hf}, device_id_type=MESH,
            ),
            pltpu.make_async_copy(rout.at[i, hf], ret.at[row], ret_sem.at[row]),
        )

    def own(i):
        for k in range(4):
            for hf in range(2):
                pltpu.make_async_remote_copy(
                    inc.at[i * 4 + k, hf], inc.at[i * 4 + k, hf],
                    dsp_sem.at[0], inc_sem.at[i * 4 + k, hf],
                    device_id=partner, device_id_type=MESH,
                ).wait_recv()
        y = dot(gather, inc[pl.ds(i * 4, 4)].reshape(big, LANES))
        hid = hidden([y[c * 8:(c + 1) * 8] for c in range(2 * chunks)], cgu_v[...], 2 * ncold)
        o = dot(hid, cd_v[...])
        o = jnp.concatenate(
            [o[:, c * LANES:(c + 1) * LANES] for c in range(2 * chunks)], axis=0
        ).astype(BF16)
        rout[pl.ds(i * 4, 4)] = dot(scatter, o).astype(BF16).reshape(4, 2, pay, LANES)
        for k in range(4):
            for hf in range(2):
                mine, remote, local = returns(i * 4 + k, hf)

                @pl.when(mine)
                def _():
                    local.start()

                @pl.when(jnp.logical_not(mine))
                def _():
                    remote.start()

    loop(n // 8, own)

    loads[7].wait()

    def hot_down(side):
        part = dot(hot_hidden, hd_v[:, pl.ds(pl.multiple_of(side * half, half), half)])
        return jnp.concatenate(
            [part[:, c * LANES:(c + 1) * LANES] for c in range(chunks)], axis=0
        )

    hot_send[...] = hot_down(other)
    send_hot = pltpu.make_async_remote_copy(
        hot_send, hot_recv, hot_sem.at[0], hot_sem.at[1], device_id=partner, device_id_type=MESH
    )
    send_hot.start()
    result = hot_down(h) + x.astype(F32)

    cold_acc[...] = result

    def collect(i):
        for k in range(4 * per):
            o = i * 4 * per + k
            pltpu.make_async_remote_copy(
                ret.at[o], ret.at[o], dsp_sem.at[0], ret_sem.at[o],
                device_id=partner, device_id_type=MESH,
            ).wait_recv()
        shape = (stack, 4 * per * pay)
        column = iota(shape, 1)
        place = jnp.full(shape, -1, jnp.int32)
        slot = lax.div(column, pay * per) * CAP + lax.rem(lax.div(column, chunks), CAP)
        for k, p in enumerate(slots(i * 4)):
            place = jnp.where(slot == k, p, place)
        line = iota(shape, 0)
        hit = jnp.logical_and(
            lax.rem(column, chunks) == lax.div(line, REQ), lax.rem(line, REQ) == place
        )
        cold_acc[...] += dot(
            onehot(hit), ret[pl.ds(i * 4 * per, 4 * per)].reshape(4 * per * pay, LANES)
        )

    loop(nb // 4, collect)
    send_hot.wait()
    result = cold_acc[...] + hot_recv[...]
    for c in range(chunks):
        out_ref[:, c * LANES:(c + 1) * LANES] = result[c * REQ:(c + 1) * REQ].astype(out_ref.dtype)

    loop(n - 1, lambda step: dispatch(step + 1).wait_send())

    @pl.when(t != h)
    def _():
        dispatch(0).wait_send()

    def drain(i):
        for hf in range(2):
            mine, remote, _ = returns(i, hf)

            @pl.when(jnp.logical_not(mine))
            def _():
                remote.wait_send()

    loop(n // 2, drain)


def local(n, residual_in, query, key_cache, value_cache, key_new, value_new, lengths, norm_gain,
          hot_gate, hot_up, hot_down, cold_gate, cold_up, cold_down, active):
    width = hot_gate.shape[1]
    half = width // 2
    chunks = half // LANES
    nb = active.shape[1]
    nhot, ncold = hot_gate.shape[0], cold_gate.shape[0]
    ctx = key_cache.shape[2]
    vmem = pl.BlockSpec(memory_space=pltpu.VMEM)
    smem = pl.BlockSpec(memory_space=pltpu.SMEM)
    hbm = pl.BlockSpec(memory_space=pl.ANY)
    pay = CAP * chunks
    dma = pltpu.SemaphoreType.DMA
    return pl.pallas_call(
        functools.partial(kernel, n, nb, ctx, nhot, ncold, width),
        out_shape=jax.ShapeDtypeStruct(residual_in.shape, residual_in.dtype),
        in_specs=[vmem] * 5 + [smem] * 2 + [hbm] * 8,
        out_specs=vmem,
        scratch_shapes=[
            pltpu.VMEM(key_cache.shape, BF16),
            pltpu.VMEM(value_cache.shape, BF16),
            pltpu.VMEM((2 * nhot, width), BF16),
            pltpu.VMEM((nhot, width), BF16),
            pltpu.VMEM((4 * ncold, width), BF16),
            pltpu.VMEM((2 * ncold, width), BF16),
            pltpu.VMEM((2, chunks * REQ, LANES), BF16),
            pltpu.VMEM((nb, pay, LANES), BF16),
            pltpu.VMEM((n // 2, 2, pay, LANES), BF16),
            pltpu.VMEM((n // 2, 2, pay, LANES), BF16),
            pltpu.VMEM((n, pay, LANES), BF16),
            pltpu.VMEM((chunks * REQ, LANES), F32),
            pltpu.VMEM((chunks * REQ, LANES), F32),
            pltpu.VMEM((chunks * REQ, LANES), F32),
            dma((8,)), dma((3,)), dma((3,)), dma((2,)), dma((2,)),
            dma((n,)), dma((n // 2, 2)), dma((n // 2, 2)), dma((n,)),
        ],
        compiler_params=pltpu.CompilerParams(
            collective_id=0, has_side_effects=True, vmem_limit_bytes=40 * 1024 * 1024
        ),
        name="decode_step",
    )(
        query, residual_in, key_new, value_new, norm_gain.reshape(1, width), lengths, active,
        key_cache, value_cache, hot_gate, hot_up, hot_down, cold_gate, cold_up, cold_down,
    )


def solution(mesh):
    return jax.shard_map(
        functools.partial(local, mesh.shape["rows"]),
        mesh=mesh,
        in_specs=(
            P(("groups", "rows"), "heads"),
            P(("groups", "rows"), "heads"),
            P(("groups", "rows"), "heads", None, None),
            P(("groups", "rows"), "heads", None, None),
            P(("groups", "rows"), "heads", None),
            P(("groups", "rows"), "heads", None),
            P(("groups", "rows")),
            P(),
            P("heads", None),
            P("heads", None),
            P("heads", None),
            P(("rows", "heads"), None),
            P(("rows", "heads"), None),
            P(("rows", "heads"), None),
            P(("groups", "rows"), None),
        ),
        out_specs=P(("groups", "rows"), "heads"),
        check_vma=False,
    )
```

```python
import functools

import jax
import jax.numpy as jnp
from jax import lax
from jax.experimental import pallas as pl
from jax.experimental.pallas import tpu as pltpu
from jax.sharding import PartitionSpec as P

HD = 128
GROUP = 16
CAP = 2
REQ = 8
LANES = 512
F32 = jnp.float32
BF16 = jnp.bfloat16
MESH = pl.DeviceIdType.MESH


def iota(shape, axis):
    return lax.broadcasted_iota(jnp.int32, shape, axis)


def div(v, k):
    return lax.shift_right_logical(v, k.bit_length() - 1) if k & (k - 1) == 0 else lax.div(v, k)


def rem(v, k):
    return v & (k - 1) if k & (k - 1) == 0 else lax.rem(v, k)


def onehot(hit):
    return jnp.where(hit, 1.0, 0.0).astype(BF16)


def dot(a, b):
    return jnp.dot(a, b, preferred_element_type=F32)


def dot_t(a, b):
    return lax.dot_general(a, b, (((1,), (1,)), ((), ())), preferred_element_type=F32)


def loop(count, body):
    if count <= 8:
        for step in range(count):
            body(step)
    else:
        lax.fori_loop(0, count, lambda step, carry: (body(step), carry)[1], 0)


def kernel(n, nb, ctx, nhot, ncold, width, *refs):
    (
        q_hbm, res_hbm, kn_hbm, vn_hbm, gain_hbm, len_hbm, act_hbm,
        kc_hbm, vc_hbm, hg_hbm, hu_hbm, hd_hbm, cg_hbm, cu_hbm, cd_hbm,
        out_ref,
        q_ref, res_ref, kn_ref, vn_ref, gain_ref, len_ref, act_ref,
        sel_v, back_v, gather_v, scatter_v,
        kc_v, vc_v, hgu_v, hd_v, cgu_v, cd_v,
        xh, dsp, inc, rout, ret, hot_send, hot_recv, cold_acc,
        load_sem, swap_send, swap_recv, x_sem, hot_sem,
        dsp_sem, inc_sem, rout_sem, ret_sem,
    ) = refs
    half = width // 2
    chunks = half // LANES
    per = n // nb
    row = lax.axis_index("rows")
    h = lax.axis_index("heads")
    other = 1 - h
    t = lax.rem(row, 2)
    idx = lax.div(row, 2)
    partner = {"heads": other}

    loads = [
        (kc_hbm, kc_v),
        (vc_hbm, vc_v),
        (cg_hbm, cgu_v.at[pl.ds(pl.multiple_of(h * ncold, ncold), ncold)]),
        (cu_hbm, cgu_v.at[pl.ds(pl.multiple_of((2 + h) * ncold, ncold), ncold)]),
        (hg_hbm, hgu_v.at[pl.ds(0, nhot)]),
        (hu_hbm, hgu_v.at[pl.ds(nhot, nhot)]),
        (cd_hbm, cd_v.at[pl.ds(pl.multiple_of(h * ncold, ncold), ncold)]),
        (hd_hbm, hd_v),
        (q_hbm, q_ref),
        (kn_hbm, kn_ref),
        (vn_hbm, vn_ref),
        (res_hbm, res_ref),
        (gain_hbm, gain_ref),
        (len_hbm, len_ref),
        (act_hbm, act_ref),
    ]
    loads = [
        pltpu.make_async_copy(src, dst, load_sem.at[i]) for i, (src, dst) in enumerate(loads)
    ]
    for i in (13, 14, 8, 0, 9, 1, 10, 11, 12, 2, 3, 4, 5, 6, 7):
        loads[i].start()

    barrier = pltpu.get_barrier_semaphore()

    def greet(step):
        peer = lax.rem(row + step, n)
        for side in range(2):
            @pl.when(jnp.logical_or(peer != row, h != side))
            def _():
                pl.semaphore_signal(
                    barrier, inc=1, device_id={"rows": peer, "heads": side}, device_id_type=MESH
                )

    loop(n, greet)

    stack = chunks * REQ
    pay = CAP * chunks
    loads[13].wait()
    loads[14].wait()

    def prepare(i):
        targets = []
        for b in range(4):
            count = jnp.int32(0)
            places = [jnp.int32(-1)] * CAP
            for r in range(REQ):
                on = act_ref[i * 4 + b, r]
                for s in range(CAP):
                    places[s] = jnp.where(
                        jnp.logical_and(on == 1, count == s), jnp.int32(r), places[s]
                    )
                count = count + on
            targets += places
        line = iota((4 * pay, 1), 0)
        target = jnp.full((4 * pay, 1), -1, jnp.int32)
        for k, p in enumerate(targets):
            target = jnp.where(div(line, chunks) == k, p, target)
        target = jnp.where(target < 0, -1, rem(line, chunks) * REQ + target)
        sel_v[i] = onehot(iota((4 * pay, stack), 1) == target)
        column = iota((1, 4 * per * pay), 1)
        slot = div(column, pay * per) * CAP + rem(div(column, chunks), CAP)
        target = jnp.full(column.shape, -1, jnp.int32)
        for k, p in enumerate(targets):
            target = jnp.where(slot == k, p, target)
        target = jnp.where(target < 0, -1, rem(column, chunks) * REQ + target)
        back_v[i] = onehot(iota((stack, 4 * per * pay), 0) == target)

    loop(nb // 4, prepare)

    big = 4 * 2 * pay

    def packed(v):
        hf, c = div(v, chunks * 8), rem(div(v, 8), chunks)
        i, s = rem(div(v, 2), 4), rem(v, 2)
        return ((i * 2 + hf) * CAP + s) * chunks + c

    gather_v[...] = onehot(packed(iota((big, 1), 0)) == iota((big, big), 1))
    scatter_v[...] = onehot(packed(iota((1, big), 1)) == iota((big, big), 0))

    scale = 1.0 / HD**0.5
    span = REQ * ctx
    rows_q = GROUP * REQ
    col = iota((1, span), 1)
    whose = jnp.full((1, span), -1, jnp.int32)
    for r in range(REQ):
        here = jnp.logical_and(col >= r * ctx, col < r * ctx + len_ref[r])
        whose = jnp.where(here, r, whose)
    mask = rem(iota((rows_q, span), 0), REQ) == whose

    pl.semaphore_wait(barrier, 2 * n - 1)
    swaps = [
        (cg_hbm, cgu_v.at[pl.ds(pl.multiple_of(h * ncold, ncold), ncold)]),
        (cu_hbm, cgu_v.at[pl.ds(pl.multiple_of((2 + h) * ncold, ncold), ncold)]),
        (cd_hbm, cd_v.at[pl.ds(pl.multiple_of(h * ncold, ncold), ncold)]),
    ]
    swaps = [
        pltpu.make_async_remote_copy(
            src, dst, swap_send.at[i], swap_recv.at[i], device_id=partner, device_id_type=MESH
        )
        for i, (src, dst) in enumerate(swaps)
    ]
    for copy in swaps:
        copy.start()
    for i in (8, 0, 9, 1, 10, 11):
        loads[i].wait()

    q = q_ref[...].astype(F32)
    kv_local = kc_v.shape[1]
    tiles = []

    def attend(g):
        qs = jnp.concatenate(
            [q[:, (g * GROUP + j) * HD:(g * GROUP + j + 1) * HD] for j in range(GROUP)], axis=0
        )
        keys = kc_v[:, g].reshape(span, HD)
        s = dot_t(qs.astype(BF16), keys) * scale
        key_own = jnp.concatenate([kn_ref[:, g, :].astype(F32)] * GROUP, axis=0)
        own = jnp.sum(qs * key_own, axis=-1, keepdims=True) * scale
        s = jnp.where(mask, s, -1e30)
        top = jnp.maximum(jnp.max(s, axis=-1, keepdims=True), own)
        e = jnp.where(mask, jnp.exp(s - top), 0.0)
        e_own = jnp.exp(own - top)
        inv = 1.0 / (jnp.sum(e, axis=-1, keepdims=True) + e_own)
        w = (e * inv).astype(BF16)
        w_own = (e_own * inv).astype(BF16).astype(F32)
        value_own = jnp.concatenate([vn_ref[:, g, :].astype(F32)] * GROUP, axis=0)
        o = dot(w, vc_v[:, g].reshape(span, HD)) + w_own * value_own
        for j in range(GROUP):
            tiles.append(o[j * REQ:(j + 1) * REQ])

    for g in range(kv_local):
        attend(g)

    per_chunk = LANES // HD
    residual = res_ref[...].astype(F32)
    x = jnp.concatenate(
        [
            residual[:, c * LANES:(c + 1) * LANES]
            + jnp.concatenate(tiles[c * per_chunk:(c + 1) * per_chunk], axis=1)
            for c in range(chunks)
        ],
        axis=0,
    ).astype(BF16)
    xh[h] = x

    def select(i):
        dsp[pl.ds(i * 4, 4)] = dot(sel_v[i], x).astype(BF16).reshape(4, pay, LANES)

    loop(nb // 4, select)

    def dispatch(step):
        dst = lax.rem(row + step, n)
        return pltpu.make_async_remote_copy(
            dsp.at[lax.div(dst, per)], inc.at[idx, h], dsp_sem.at[step], inc_sem.at[idx, h],
            device_id={"rows": dst, "heads": t}, device_id_type=MESH,
        )

    dispatch_own = pltpu.make_async_copy(
        dsp.at[lax.div(row, per)], inc.at[idx, h], inc_sem.at[idx, h]
    )
    loop(n - 1, lambda step: dispatch(step + 1).start())

    @pl.when(t == h)
    def _():
        dispatch_own.start()

    @pl.when(t != h)
    def _():
        dispatch(0).start()

    send_x = pltpu.make_async_remote_copy(
        xh.at[h], xh.at[h], x_sem.at[0], x_sem.at[1], device_id=partner, device_id_type=MESH
    )
    send_x.start()

    def hidden(blocks, weights, count):
        total = blocks[0] * blocks[0]
        for block in blocks[1:]:
            total = total + block * block
        rs = lax.rsqrt(jnp.sum(total, axis=-1, keepdims=True) / width + 1e-05)
        normed = jnp.concatenate(
            [
                (
                    block * rs * gain_ref[c * LANES:(c + 1) * LANES].astype(F32)[None, :]
                ).astype(BF16)
                for c, block in enumerate(blocks)
            ],
            axis=1,
        )
        both = dot_t(normed, weights)
        gate, up = both[:, :count], both[:, count:]
        return (gate / (1.0 + jnp.exp(-gate)) * up).astype(BF16)

    loads[4].wait()
    loads[5].wait()
    loads[12].wait()
    send_x.wait()
    whole = [xh[side].astype(F32) for side in range(2)]
    hot_hidden = hidden(
        [whole[c // chunks][(c % chunks) * REQ:(c % chunks + 1) * REQ] for c in range(2 * chunks)],
        hgu_v[...],
        nhot,
    )

    loads[2].wait()
    loads[3].wait()
    loads[6].wait()
    for copy in swaps:
        copy.wait()

    def back(i, hf):
        return pltpu.make_async_remote_copy(
            rout.at[i, hf], ret.at[row], rout_sem.at[i, hf], ret_sem.at[row],
            device_id={"rows": 2 * i + h, "heads": hf}, device_id_type=MESH,
        )

    def mine(i, hf):
        return jnp.logical_and(2 * i + h == row, hf == h)

    def own(i):
        for k in range(4):
            for hf in range(2):
                pltpu.make_async_remote_copy(
                    inc.at[i * 4 + k, hf], inc.at[i * 4 + k, hf],
                    dsp_sem.at[0], inc_sem.at[i * 4 + k, hf],
                    device_id=partner, device_id_type=MESH,
                ).wait_recv()
        y = dot(gather_v[...], inc[pl.ds(i * 4, 4)].reshape(big, LANES))
        hid = hidden([y[c * 8:(c + 1) * 8] for c in range(2 * chunks)], cgu_v[...], 2 * ncold)
        o = dot(hid, cd_v[...])
        o = jnp.concatenate(
            [o[:, c * LANES:(c + 1) * LANES] for c in range(2 * chunks)], axis=0
        ).astype(BF16)
        rout[pl.ds(i * 4, 4)] = dot(scatter_v[...], o).astype(BF16).reshape(4, 2, pay, LANES)
        for k in range(4):
            for hf in range(2):
                @pl.when(mine(i * 4 + k, hf))
                def _():
                    pltpu.make_async_copy(
                        rout.at[i * 4 + k, hf], ret.at[row], ret_sem.at[row]
                    ).start()

                @pl.when(jnp.logical_not(mine(i * 4 + k, hf)))
                def _():
                    back(i * 4 + k, hf).start()

    loop(n // 8, own)

    loads[7].wait()

    def hot_down(side):
        part = dot(hot_hidden, hd_v[:, pl.ds(pl.multiple_of(side * half, half), half)])
        return jnp.concatenate(
            [part[:, c * LANES:(c + 1) * LANES] for c in range(chunks)], axis=0
        )

    hot_send[...] = hot_down(other)
    send_hot = pltpu.make_async_remote_copy(
        hot_send, hot_recv, hot_sem.at[0], hot_sem.at[1], device_id=partner, device_id_type=MESH
    )
    send_hot.start()
    result = hot_down(h) + x.astype(F32)

    cold_acc[...] = result

    def collect(i):
        for k in range(4 * per):
            o = i * 4 * per + k
            pltpu.make_async_remote_copy(
                ret.at[o], ret.at[o], dsp_sem.at[0], ret_sem.at[o],
                device_id=partner, device_id_type=MESH,
            ).wait_recv()
        cold_acc[...] += dot(
            back_v[i], ret[pl.ds(i * 4 * per, 4 * per)].reshape(4 * per * pay, LANES)
        )

    loop(nb // 4, collect)
    send_hot.wait()
    result = cold_acc[...] + hot_recv[...]
    for c in range(chunks):
        out_ref[:, c * LANES:(c + 1) * LANES] = result[c * REQ:(c + 1) * REQ].astype(out_ref.dtype)

    loop(n - 1, lambda step: dispatch(step + 1).wait_send())

    @pl.when(t != h)
    def _():
        dispatch(0).wait_send()

    def drain(i):
        for hf in range(2):
            @pl.when(jnp.logical_not(mine(i, hf)))
            def _():
                back(i, hf).wait_send()

    loop(n // 2, drain)


def local(n, residual_in, query, key_cache, value_cache, key_new, value_new, lengths, norm_gain,
          hot_gate, hot_up, hot_down, cold_gate, cold_up, cold_down, active):
    width = hot_gate.shape[1]
    half = width // 2
    chunks = half // LANES
    nb = active.shape[1]
    nhot, ncold = hot_gate.shape[0], cold_gate.shape[0]
    ctx = key_cache.shape[2]
    vmem = pl.BlockSpec(memory_space=pltpu.VMEM)
    hbm = pl.BlockSpec(memory_space=pltpu.HBM)
    pay = CAP * chunks
    dma = pltpu.SemaphoreType.DMA
    return pl.pallas_call(
        functools.partial(kernel, n, nb, ctx, nhot, ncold, width),
        out_shape=jax.ShapeDtypeStruct(residual_in.shape, residual_in.dtype),
        in_specs=[hbm] * 15,
        out_specs=vmem,
        scratch_shapes=[
            pltpu.VMEM(query.shape, BF16),
            pltpu.VMEM(residual_in.shape, BF16),
            pltpu.VMEM(key_new.shape, BF16),
            pltpu.VMEM(value_new.shape, BF16),
            pltpu.VMEM(norm_gain.shape, BF16),
            pltpu.SMEM(lengths.shape, jnp.int32),
            pltpu.SMEM(active.shape[::-1], jnp.int32),
            pltpu.VMEM((nb // 4, 4 * pay, chunks * REQ), BF16),
            pltpu.VMEM((nb // 4, chunks * REQ, 4 * (n // nb) * pay), BF16),
            pltpu.VMEM((8 * pay, 8 * pay), BF16),
            pltpu.VMEM((8 * pay, 8 * pay), BF16),
            pltpu.VMEM(key_cache.shape, BF16),
            pltpu.VMEM(value_cache.shape, BF16),
            pltpu.VMEM((2 * nhot, width), BF16),
            pltpu.VMEM((nhot, width), BF16),
            pltpu.VMEM((4 * ncold, width), BF16),
            pltpu.VMEM((2 * ncold, width), BF16),
            pltpu.VMEM((2, chunks * REQ, LANES), BF16),
            pltpu.VMEM((nb, pay, LANES), BF16),
            pltpu.VMEM((n // 2, 2, pay, LANES), BF16),
            pltpu.VMEM((n // 2, 2, pay, LANES), BF16),
            pltpu.VMEM((n, pay, LANES), BF16),
            pltpu.VMEM((chunks * REQ, LANES), F32),
            pltpu.VMEM((chunks * REQ, LANES), F32),
            pltpu.VMEM((chunks * REQ, LANES), F32),
            dma((15,)), dma((3,)), dma((3,)), dma((2,)), dma((2,)),
            dma((n,)), dma((n // 2, 2)), dma((n // 2, 2)), dma((n,)),
        ],
        compiler_params=pltpu.CompilerParams(
            collective_id=0, has_side_effects=True, vmem_limit_bytes=64 * 1024 * 1024
        ),
        name="decode_step",
    )(
        query, residual_in, key_new, value_new, norm_gain, lengths, active.T,
        key_cache, value_cache, hot_gate, hot_up, hot_down, cold_gate, cold_up, cold_down,
    )


def solution(mesh):
    return jax.shard_map(
        functools.partial(local, mesh.shape["rows"]),
        mesh=mesh,
        in_specs=(
            P(("groups", "rows"), "heads"),
            P(("groups", "rows"), "heads"),
            P(("groups", "rows"), "heads", None, None),
            P(("groups", "rows"), "heads", None, None),
            P(("groups", "rows"), "heads", None),
            P(("groups", "rows"), "heads", None),
            P(("groups", "rows")),
            P(),
            P("heads", None),
            P("heads", None),
            P("heads", None),
            P(("rows", "heads"), None),
            P(("rows", "heads"), None),
            P(("rows", "heads"), None),
            P(("groups", "rows"), None),
        ),
        out_specs=P(("groups", "rows"), "heads"),
        check_vma=False,
    )
```

```python
import functools

import jax
import jax.numpy as jnp
from jax import lax
from jax.experimental import pallas as pl
from jax.experimental.pallas import tpu as pltpu
from jax.sharding import PartitionSpec as P

HD = 128
GROUP = 16
CAP = 2
REQ = 8
LANES = 512
F32 = jnp.float32
BF16 = jnp.bfloat16
MESH = pl.DeviceIdType.MESH


def iota(shape, axis):
    return lax.broadcasted_iota(jnp.int32, shape, axis)


def div(v, k):
    return lax.shift_right_logical(v, k.bit_length() - 1) if k & (k - 1) == 0 else lax.div(v, k)


def rem(v, k):
    return v & (k - 1) if k & (k - 1) == 0 else lax.rem(v, k)


def onehot(hit):
    return jnp.where(hit, 1.0, 0.0).astype(BF16)


def dot(a, b):
    return jnp.dot(a, b, preferred_element_type=F32)


def dot_t(a, b):
    return lax.dot_general(a, b, (((1,), (1,)), ((), ())), preferred_element_type=F32)


def loop(count, body):
    if count <= 8:
        for step in range(count):
            body(step)
    else:
        lax.fori_loop(0, count, lambda step, carry: (body(step), carry)[1], 0)


def kernel(n, nb, ctx, nhot, ncold, width, *refs):
    (
        q_hbm, res_hbm, kn_hbm, vn_hbm, gain_hbm, len_hbm, act_hbm,
        kc_hbm, vc_hbm, hg_hbm, hu_hbm, hd_hbm, cg_hbm, cu_hbm, cd_hbm,
        out_ref,
        q_ref, res_ref, kn_ref, vn_ref, gain_ref, len_ref, act_ref,
        sel_v, back_v, gather_v, scatter_v,
        kc_v, vc_v, hgu_v, hd_v, cgu_v, cd_v,
        xh, dsp, inc, rout, ret, hot_send, hot_recv, cold_acc,
        load_sem, swap_send, swap_recv, x_sem, hot_sem,
        dsp_sem, inc_sem, rout_sem, ret_sem,
    ) = refs
    half = width // 2
    chunks = half // LANES
    per = n // nb
    row = lax.axis_index("rows")
    h = lax.axis_index("heads")
    other = 1 - h
    t = lax.rem(row, 2)
    idx = lax.div(row, 2)
    partner = {"heads": other}

    loads = [
        (kc_hbm, kc_v),
        (vc_hbm, vc_v),
        (cg_hbm, cgu_v.at[pl.ds(pl.multiple_of(h * ncold, ncold), ncold)]),
        (cu_hbm, cgu_v.at[pl.ds(pl.multiple_of((2 + h) * ncold, ncold), ncold)]),
        (hg_hbm, hgu_v.at[pl.ds(0, nhot)]),
        (hu_hbm, hgu_v.at[pl.ds(nhot, nhot)]),
        (cd_hbm, cd_v.at[pl.ds(pl.multiple_of(h * ncold, ncold), ncold)]),
        (hd_hbm, hd_v),
        (q_hbm, q_ref),
        (kn_hbm, kn_ref),
        (vn_hbm, vn_ref),
        (res_hbm, res_ref),
        (gain_hbm, gain_ref),
        (len_hbm, len_ref),
        (act_hbm, act_ref),
    ]
    loads = [
        pltpu.make_async_copy(src, dst, load_sem.at[i]) for i, (src, dst) in enumerate(loads)
    ]
    for i in (14, 13, 8, 0, 9, 1, 10, 11, 12):
        loads[i].start()

    barrier = pltpu.get_barrier_semaphore()

    def greet(step):
        peer = lax.rem(row + step, n)
        for side in range(2):
            @pl.when(jnp.logical_or(peer != row, h != side))
            def _():
                pl.semaphore_signal(
                    barrier, inc=1, device_id={"rows": peer, "heads": side}, device_id_type=MESH
                )

    loop(n, greet)

    stack = chunks * REQ
    pay = CAP * chunks
    loads[13].wait()
    loads[14].wait()

    def prepare(i):
        targets = []
        for b in range(4):
            count = jnp.int32(0)
            places = [jnp.int32(-1)] * CAP
            for r in range(REQ):
                on = act_ref[i * 4 + b, r]
                for s in range(CAP):
                    places[s] = jnp.where(
                        jnp.logical_and(on == 1, count == s), jnp.int32(r), places[s]
                    )
                count = count + on
            targets += places
        line = iota((4 * pay, 1), 0)
        target = jnp.full((4 * pay, 1), -1, jnp.int32)
        for k, p in enumerate(targets):
            target = jnp.where(div(line, chunks) == k, p, target)
        target = jnp.where(target < 0, -1, rem(line, chunks) * REQ + target)
        sel_v[i] = onehot(iota((4 * pay, stack), 1) == target)
        column = iota((1, 4 * per * pay), 1)
        slot = div(column, pay * per) * CAP + rem(div(column, chunks), CAP)
        target = jnp.full(column.shape, -1, jnp.int32)
        for k, p in enumerate(targets):
            target = jnp.where(slot == k, p, target)
        target = jnp.where(target < 0, -1, rem(column, chunks) * REQ + target)
        back_v[i] = onehot(iota((stack, 4 * per * pay), 0) == target)

    loop(nb // 4, prepare)

    big = 4 * 2 * pay

    def packed(v):
        hf, c = div(v, chunks * 8), rem(div(v, 8), chunks)
        i, s = rem(div(v, 2), 4), rem(v, 2)
        return ((i * 2 + hf) * CAP + s) * chunks + c

    gather_v[...] = onehot(packed(iota((big, 1), 0)) == iota((big, big), 1))
    scatter_v[...] = onehot(packed(iota((1, big), 1)) == iota((big, big), 0))

    scale = 1.0 / HD**0.5
    span = REQ * ctx
    rows_q = GROUP * REQ
    col = iota((1, span), 1)
    whose = jnp.full((1, span), -1, jnp.int32)
    for r in range(REQ):
        here = jnp.logical_and(col >= r * ctx, col < r * ctx + len_ref[r])
        whose = jnp.where(here, r, whose)
    mask = rem(iota((rows_q, span), 0), REQ) == whose

    for i in (2, 3, 6, 4, 5, 7):
        loads[i].start()
    pl.semaphore_wait(barrier, 2 * n - 1)
    swaps = [
        (cg_hbm, cgu_v.at[pl.ds(pl.multiple_of(h * ncold, ncold), ncold)]),
        (cu_hbm, cgu_v.at[pl.ds(pl.multiple_of((2 + h) * ncold, ncold), ncold)]),
        (cd_hbm, cd_v.at[pl.ds(pl.multiple_of(h * ncold, ncold), ncold)]),
    ]
    swaps = [
        pltpu.make_async_remote_copy(
            src, dst, swap_send.at[i], swap_recv.at[i], device_id=partner, device_id_type=MESH
        )
        for i, (src, dst) in enumerate(swaps)
    ]
    for copy in swaps:
        copy.start()
    for i in (8, 0, 9, 1, 10, 11):
        loads[i].wait()

    q = q_ref[...].astype(F32)
    kv_local = kc_v.shape[1]
    tiles = []

    def attend(g):
        qs = jnp.concatenate(
            [q[:, (g * GROUP + j) * HD:(g * GROUP + j + 1) * HD] for j in range(GROUP)], axis=0
        )
        keys = kc_v[:, g].reshape(span, HD)
        s = dot_t(qs.astype(BF16), keys) * scale
        key_own = jnp.concatenate([kn_ref[:, g, :].astype(F32)] * GROUP, axis=0)
        own = jnp.sum(qs * key_own, axis=-1, keepdims=True) * scale
        s = jnp.where(mask, s, -1e30)
        top = jnp.maximum(jnp.max(s, axis=-1, keepdims=True), own)
        e = jnp.where(mask, jnp.exp(s - top), 0.0)
        e_own = jnp.exp(own - top)
        inv = 1.0 / (jnp.sum(e, axis=-1, keepdims=True) + e_own)
        value_own = jnp.concatenate([vn_ref[:, g, :].astype(F32)] * GROUP, axis=0)
        o = (dot(e.astype(BF16), vc_v[:, g].reshape(span, HD)) + e_own * value_own) * inv
        for j in range(GROUP):
            tiles.append(o[j * REQ:(j + 1) * REQ])

    for g in range(kv_local):
        attend(g)

    per_chunk = LANES // HD
    residual = res_ref[...].astype(F32)
    x = jnp.concatenate(
        [
            residual[:, c * LANES:(c + 1) * LANES]
            + jnp.concatenate(tiles[c * per_chunk:(c + 1) * per_chunk], axis=1)
            for c in range(chunks)
        ],
        axis=0,
    ).astype(BF16)
    xh[h] = x

    def select(i):
        dsp[pl.ds(i * 4, 4)] = dot(sel_v[i], x).astype(BF16).reshape(4, pay, LANES)

    loop(nb // 4, select)

    def dispatch(step):
        dst = lax.rem(row + step, n)
        return pltpu.make_async_remote_copy(
            dsp.at[lax.div(dst, per)], inc.at[idx, h], dsp_sem.at[step], inc_sem.at[idx, h],
            device_id={"rows": dst, "heads": t}, device_id_type=MESH,
        )

    dispatch_own = pltpu.make_async_copy(
        dsp.at[lax.div(row, per)], inc.at[idx, h], inc_sem.at[idx, h]
    )
    loop(n - 1, lambda step: dispatch(step + 1).start())

    @pl.when(t == h)
    def _():
        dispatch_own.start()

    @pl.when(t != h)
    def _():
        dispatch(0).start()

    send_x = pltpu.make_async_remote_copy(
        xh.at[h], xh.at[h], x_sem.at[0], x_sem.at[1], device_id=partner, device_id_type=MESH
    )
    send_x.start()

    def hidden(blocks, weights, count):
        total = blocks[0] * blocks[0]
        for block in blocks[1:]:
            total = total + block * block
        rs = lax.rsqrt(jnp.sum(total, axis=-1, keepdims=True) / width + 1e-05)
        normed = jnp.concatenate(
            [
                (
                    block * gain_ref[c * LANES:(c + 1) * LANES].astype(F32)[None, :]
                ).astype(BF16)
                for c, block in enumerate(blocks)
            ],
            axis=1,
        )
        both = dot_t(normed, weights) * rs
        gate, up = both[:, :count], both[:, count:]
        return (gate / (1.0 + jnp.exp(-gate)) * up).astype(BF16)

    loads[4].wait()
    loads[5].wait()
    loads[12].wait()
    send_x.wait()
    whole = [xh[side].astype(F32) for side in range(2)]
    hot_hidden = hidden(
        [whole[c // chunks][(c % chunks) * REQ:(c % chunks + 1) * REQ] for c in range(2 * chunks)],
        hgu_v[...],
        nhot,
    )

    loads[2].wait()
    loads[3].wait()
    loads[6].wait()
    for copy in swaps:
        copy.wait()

    def back(i, hf):
        return pltpu.make_async_remote_copy(
            rout.at[i, hf], ret.at[row], rout_sem.at[i, hf], ret_sem.at[row],
            device_id={"rows": 2 * i + h, "heads": hf}, device_id_type=MESH,
        )

    def mine(i, hf):
        return jnp.logical_and(2 * i + h == row, hf == h)

    def own(i):
        for k in range(4):
            for hf in range(2):
                pltpu.make_async_remote_copy(
                    inc.at[i * 4 + k, hf], inc.at[i * 4 + k, hf],
                    dsp_sem.at[0], inc_sem.at[i * 4 + k, hf],
                    device_id=partner, device_id_type=MESH,
                ).wait_recv()
        y = dot(gather_v[...], inc[pl.ds(i * 4, 4)].reshape(big, LANES))
        hid = hidden([y[c * 8:(c + 1) * 8] for c in range(2 * chunks)], cgu_v[...], 2 * ncold)
        o = dot(hid, cd_v[...])
        o = jnp.concatenate(
            [o[:, c * LANES:(c + 1) * LANES] for c in range(2 * chunks)], axis=0
        ).astype(BF16)
        rout[pl.ds(i * 4, 4)] = dot(scatter_v[...], o).astype(BF16).reshape(4, 2, pay, LANES)
        for k in range(4):
            far = i * 4 + jnp.where(idx < n // 4, 3 - k, k)
            for hf in range(2):
                @pl.when(mine(far, hf))
                def _():
                    pltpu.make_async_copy(rout.at[far, hf], ret.at[row], ret_sem.at[row]).start()

                @pl.when(jnp.logical_not(mine(far, hf)))
                def _():
                    back(far, hf).start()

    loop(n // 8, own)

    loads[7].wait()

    def hot_down(side):
        part = dot(hot_hidden, hd_v[:, pl.ds(pl.multiple_of(side * half, half), half)])
        return jnp.concatenate(
            [part[:, c * LANES:(c + 1) * LANES] for c in range(chunks)], axis=0
        )

    hot_send[...] = hot_down(other)
    send_hot = pltpu.make_async_remote_copy(
        hot_send, hot_recv, hot_sem.at[0], hot_sem.at[1], device_id=partner, device_id_type=MESH
    )
    send_hot.start()
    result = hot_down(h) + x.astype(F32)

    cold_acc[...] = result

    def collect(i):
        for k in range(4 * per):
            o = i * 4 * per + k
            pltpu.make_async_remote_copy(
                ret.at[o], ret.at[o], dsp_sem.at[0], ret_sem.at[o],
                device_id=partner, device_id_type=MESH,
            ).wait_recv()
        cold_acc[...] += dot(
            back_v[i], ret[pl.ds(i * 4 * per, 4 * per)].reshape(4 * per * pay, LANES)
        )

    loop(nb // 4, collect)
    send_hot.wait()
    result = cold_acc[...] + hot_recv[...]
    for c in range(chunks):
        out_ref[:, c * LANES:(c + 1) * LANES] = result[c * REQ:(c + 1) * REQ].astype(out_ref.dtype)

    loop(n - 1, lambda step: dispatch(step + 1).wait_send())

    @pl.when(t != h)
    def _():
        dispatch(0).wait_send()

    def drain(i):
        for hf in range(2):
            @pl.when(jnp.logical_not(mine(i, hf)))
            def _():
                back(i, hf).wait_send()

    loop(n // 2, drain)


def local(n, residual_in, query, key_cache, value_cache, key_new, value_new, lengths, norm_gain,
          hot_gate, hot_up, hot_down, cold_gate, cold_up, cold_down, active):
    width = hot_gate.shape[1]
    half = width // 2
    chunks = half // LANES
    nb = active.shape[1]
    nhot, ncold = hot_gate.shape[0], cold_gate.shape[0]
    ctx = key_cache.shape[2]
    vmem = pl.BlockSpec(memory_space=pltpu.VMEM)
    hbm = pl.BlockSpec(memory_space=pltpu.HBM)
    pay = CAP * chunks
    dma = pltpu.SemaphoreType.DMA
    return pl.pallas_call(
        functools.partial(kernel, n, nb, ctx, nhot, ncold, width),
        out_shape=pltpu.VMEM(residual_in.shape, residual_in.dtype),
        in_specs=[hbm] * 15,
        out_specs=vmem,
        scratch_shapes=[
            pltpu.VMEM(query.shape, BF16),
            pltpu.VMEM(residual_in.shape, BF16),
            pltpu.VMEM(key_new.shape, BF16),
            pltpu.VMEM(value_new.shape, BF16),
            pltpu.VMEM(norm_gain.shape, BF16),
            pltpu.SMEM(lengths.shape, jnp.int32),
            pltpu.SMEM(active.shape[::-1], jnp.int32),
            pltpu.VMEM((nb // 4, 4 * pay, chunks * REQ), BF16),
            pltpu.VMEM((nb // 4, chunks * REQ, 4 * (n // nb) * pay), BF16),
            pltpu.VMEM((8 * pay, 8 * pay), BF16),
            pltpu.VMEM((8 * pay, 8 * pay), BF16),
            pltpu.VMEM(key_cache.shape, BF16),
            pltpu.VMEM(value_cache.shape, BF16),
            pltpu.VMEM((2 * nhot, width), BF16),
            pltpu.VMEM((nhot, width), BF16),
            pltpu.VMEM((4 * ncold, width), BF16),
            pltpu.VMEM((2 * ncold, width), BF16),
            pltpu.VMEM((2, chunks * REQ, LANES), BF16),
            pltpu.VMEM((nb, pay, LANES), BF16),
            pltpu.VMEM((n // 2, 2, pay, LANES), BF16),
            pltpu.VMEM((n // 2, 2, pay, LANES), BF16),
            pltpu.VMEM((n, pay, LANES), BF16),
            pltpu.VMEM((chunks * REQ, LANES), F32),
            pltpu.VMEM((chunks * REQ, LANES), F32),
            pltpu.VMEM((chunks * REQ, LANES), F32),
            dma((15,)), dma((3,)), dma((3,)), dma((2,)), dma((2,)),
            dma((n,)), dma((n // 2, 2)), dma((n // 2, 2)), dma((n,)),
        ],
        compiler_params=pltpu.CompilerParams(
            collective_id=0, has_side_effects=True, vmem_limit_bytes=48 * 1024 * 1024
        ),
        name="decode_step",
    )(*[
        pltpu.with_memory_space_constraint(array, pltpu.HBM)
        for array in (
            query, residual_in, key_new, value_new, norm_gain, lengths, active.T,
            key_cache, value_cache, hot_gate, hot_up, hot_down, cold_gate, cold_up, cold_down,
        )
    ])


def solution(mesh):
    return jax.shard_map(
        functools.partial(local, mesh.shape["rows"]),
        mesh=mesh,
        in_specs=(
            P(("groups", "rows"), "heads"),
            P(("groups", "rows"), "heads"),
            P(("groups", "rows"), "heads", None, None),
            P(("groups", "rows"), "heads", None, None),
            P(("groups", "rows"), "heads", None),
            P(("groups", "rows"), "heads", None),
            P(("groups", "rows")),
            P(),
            P("heads", None),
            P("heads", None),
            P("heads", None),
            P(("rows", "heads"), None),
            P(("rows", "heads"), None),
            P(("rows", "heads"), None),
            P(("groups", "rows"), None),
        ),
        out_specs=P(("groups", "rows"), "heads"),
        check_vma=False,
    )
```

```python
import functools

import jax
import jax.numpy as jnp
from jax import lax
from jax.experimental import pallas as pl
from jax.experimental.pallas import tpu as pltpu
from jax.sharding import PartitionSpec as P

HD = 128
GROUP = 16
CAP = 2
REQ = 8
LANES = 512
F32 = jnp.float32
BF16 = jnp.bfloat16
MESH = pl.DeviceIdType.MESH


def iota(shape, axis):
    return lax.broadcasted_iota(jnp.int32, shape, axis)


def div(v, k):
    return lax.shift_right_logical(v, k.bit_length() - 1) if k & (k - 1) == 0 else lax.div(v, k)


def rem(v, k):
    return v & (k - 1) if k & (k - 1) == 0 else lax.rem(v, k)


def onehot(hit):
    return jnp.where(hit, 1.0, 0.0).astype(BF16)


def dot(a, b):
    return jnp.dot(a, b, preferred_element_type=F32)


def dot_t(a, b):
    return lax.dot_general(a, b, (((1,), (1,)), ((), ())), preferred_element_type=F32)


def loop(count, body):
    if count <= 8:
        for step in range(count):
            body(step)
    else:
        lax.fori_loop(0, count, lambda step, carry: (body(step), carry)[1], 0)


def kernel(n, nb, ctx, nhot, ncold, width, *refs):
    (
        q_hbm, res_hbm, kn_hbm, vn_hbm, gain_hbm, len_hbm, act_hbm,
        kc_hbm, vc_hbm, hg_hbm, hu_hbm, hd_hbm, cg_hbm, cu_hbm, cd_hbm,
        out_ref,
        q_ref, res_ref, kn_ref, vn_ref, gain_ref, len_ref, act_ref,
        sel_v, back_v, gather_v, scatter_v, hid_v,
        kc_v, vc_v, hgu_v, hd_v, cgu_v, cd_v,
        xh, dsp, inc, rout, ret, hot_send, hot_recv, cold_acc,
        load_sem, swap_send, swap_recv, x_sem, hot_sem,
        dsp_sem, inc_sem, rout_sem, ret_sem,
    ) = refs
    half = width // 2
    chunks = half // LANES
    per = n // nb
    row = lax.axis_index("rows")
    h = lax.axis_index("heads")
    other = 1 - h
    t = lax.rem(row, 2)
    idx = lax.div(row, 2)
    partner = {"heads": other}

    loads = [
        (kc_hbm, kc_v),
        (vc_hbm, vc_v),
        (cg_hbm, cgu_v.at[pl.ds(pl.multiple_of(h * ncold, ncold), ncold)]),
        (cu_hbm, cgu_v.at[pl.ds(pl.multiple_of((2 + h) * ncold, ncold), ncold)]),
        (hg_hbm, hgu_v.at[pl.ds(0, nhot)]),
        (hu_hbm, hgu_v.at[pl.ds(nhot, nhot)]),
        (cd_hbm, cd_v.at[pl.ds(pl.multiple_of(h * ncold, ncold), ncold)]),
        (hd_hbm, hd_v),
        (q_hbm, q_ref),
        (kn_hbm, kn_ref),
        (vn_hbm, vn_ref),
        (res_hbm, res_ref),
        (gain_hbm, gain_ref),
        (len_hbm, len_ref),
        (act_hbm, act_ref),
    ]
    loads = [
        pltpu.make_async_copy(src, dst, load_sem.at[i]) for i, (src, dst) in enumerate(loads)
    ]
    for i in (14, 13, 8, 0, 9, 1, 10, 11, 12):
        loads[i].start()

    barrier = pltpu.get_barrier_semaphore()

    def greet(step):
        peer = lax.rem(row + step + 1, n)
        for side in range(2):
            pl.semaphore_signal(
                barrier, inc=1, device_id={"rows": peer, "heads": side}, device_id_type=MESH
            )

    pl.semaphore_signal(barrier, inc=1, device_id=partner, device_id_type=MESH)
    loop(n - 1, greet)

    stack = chunks * REQ
    pay = CAP * chunks
    loads[13].wait()
    loads[14].wait()

    def prepare(i):
        targets = []
        for b in range(4):
            count = jnp.int32(0)
            places = [jnp.int32(-1)] * CAP
            for r in range(REQ):
                on = act_ref[i * 4 + b, r]
                for s in range(CAP):
                    places[s] = jnp.where(
                        jnp.logical_and(on == 1, count == s), jnp.int32(r), places[s]
                    )
                count = count + on
            targets += places
        line = iota((4 * pay, 1), 0)
        target = jnp.full((4 * pay, 1), -1, jnp.int32)
        for k, p in enumerate(targets):
            target = jnp.where(div(line, chunks) == k, p, target)
        target = jnp.where(target < 0, -1, rem(line, chunks) * REQ + target)
        sel_v[i] = onehot(iota((4 * pay, stack), 1) == target)
        column = iota((1, 4 * per * pay), 1)
        slot = div(column, pay * per) * CAP + rem(div(column, chunks), CAP)
        target = jnp.full(column.shape, -1, jnp.int32)
        for k, p in enumerate(targets):
            target = jnp.where(slot == k, p, target)
        target = jnp.where(target < 0, -1, rem(column, chunks) * REQ + target)
        back_v[i] = onehot(iota((stack, 4 * per * pay), 0) == target)

    loop(nb // 4, prepare)

    big = 4 * pay

    def packed(v):
        return rem(v, 8) * chunks + div(v, 8)

    gather_v[...] = onehot(packed(iota((big, 1), 0)) == iota((big, big), 1))
    scatter_v[...] = onehot(packed(iota((1, big), 1)) == iota((big, big), 0))
    for i in (2, 3, 6, 4, 5, 7):
        loads[i].start()

    scale = 1.0 / HD**0.5
    span = REQ * ctx
    rows_q = GROUP * REQ
    col = iota((1, span + HD), 1)
    whose = jnp.where(jnp.logical_and(col >= span, col < span + REQ), col - span, -1)
    for r in range(REQ):
        here = jnp.logical_and(col >= r * ctx, col < r * ctx + len_ref[r])
        whose = jnp.where(here, r, whose)
    mask = rem(iota((rows_q, span + HD), 0), REQ) == whose
    blank = jnp.zeros((HD - REQ, HD), F32)
    ones = jnp.ones((span + HD, HD), BF16)
    for i in (8, 0, 9, 1, 10, 11):
        loads[i].wait()

    q = q_ref[...].astype(F32)
    kv_local = kc_v.shape[1]
    tiles = []

    def attend(g):
        qs = jnp.concatenate(
            [q[:, (g * GROUP + j) * HD:(g * GROUP + j + 1) * HD] for j in range(GROUP)], axis=0
        )
        key_own = jnp.concatenate([kn_ref[:, g, :].astype(F32), blank], axis=0).astype(BF16)
        keys = jnp.concatenate([kc_v[:, g].reshape(span, HD), key_own], axis=0)
        s = jnp.where(mask, dot_t(qs.astype(BF16), keys) * scale, -1e30)
        e = jnp.exp(s - jnp.max(s, axis=-1, keepdims=True))
        value_own = jnp.concatenate([vn_ref[:, g, :].astype(F32), blank], axis=0).astype(BF16)
        values = jnp.concatenate([vc_v[:, g].reshape(span, HD), value_own], axis=0)
        o = dot(e.astype(BF16), jnp.concatenate([values, ones], axis=1))
        o = o[:, :HD] / o[:, HD:]
        for j in range(GROUP):
            tiles.append(o[j * REQ:(j + 1) * REQ])

    for g in range(kv_local):
        attend(g)

    per_chunk = LANES // HD
    residual = res_ref[...].astype(F32)
    x = jnp.concatenate(
        [
            residual[:, c * LANES:(c + 1) * LANES]
            + jnp.concatenate(tiles[c * per_chunk:(c + 1) * per_chunk], axis=1)
            for c in range(chunks)
        ],
        axis=0,
    ).astype(BF16)
    xh[h] = x

    def select(i):
        dsp[pl.ds(i * 4, 4)] = dot(sel_v[i], x).astype(BF16).reshape(4, pay, LANES)

    loop(nb // 4, select)

    pl.semaphore_wait(barrier, 2 * n - 1)

    side = n // 2

    def dispatch(step):
        dst = lax.rem(row + step, n)
        return pltpu.make_async_remote_copy(
            dsp.at[lax.div(dst, per)], inc.at[h * side + idx], dsp_sem, inc_sem,
            device_id={"rows": dst, "heads": t}, device_id_type=MESH,
        )

    loop(n - 1, lambda step: dispatch(step + 1).start())

    @pl.when(t == h)
    def _():
        pltpu.make_async_copy(dsp.at[lax.div(row, per)], inc.at[h * side + idx], inc_sem).start()

    @pl.when(t != h)
    def _():
        dispatch(0).start()

    send_x = pltpu.make_async_remote_copy(
        xh.at[h], xh.at[h], x_sem.at[0], x_sem.at[1], device_id=partner, device_id_type=MESH
    )
    send_x.start()
    swaps = [
        (cg_hbm, cgu_v.at[pl.ds(pl.multiple_of(h * ncold, ncold), ncold)]),
        (cu_hbm, cgu_v.at[pl.ds(pl.multiple_of((2 + h) * ncold, ncold), ncold)]),
        (cd_hbm, cd_v.at[pl.ds(pl.multiple_of(h * ncold, ncold), ncold)]),
    ]
    swaps = [
        pltpu.make_async_remote_copy(
            src, dst, swap_send.at[i], swap_recv.at[i], device_id=partner, device_id_type=MESH
        )
        for i, (src, dst) in enumerate(swaps)
    ]
    for copy in swaps:
        copy.start()

    def hidden(blocks, weights, count):
        total = blocks[0] * blocks[0]
        for block in blocks[1:]:
            total = total + block * block
        rs = lax.rsqrt(jnp.sum(total, axis=-1, keepdims=True) / width + 1e-05)
        normed = jnp.concatenate(
            [
                (
                    block * gain_ref[c * LANES:(c + 1) * LANES].astype(F32)[None, :]
                ).astype(BF16)
                for c, block in enumerate(blocks)
            ],
            axis=1,
        )
        both = dot_t(normed, weights) * rs
        gate, up = both[:, :count], both[:, count:]
        return (gate / (1.0 + jnp.exp(-gate)) * up).astype(BF16)

    loads[4].wait()
    loads[5].wait()
    loads[12].wait()
    send_x.wait()
    whole = [xh[side].astype(F32) for side in range(2)]
    hot_hidden = hidden(
        [whole[c // chunks][(c % chunks) * REQ:(c % chunks + 1) * REQ] for c in range(2 * chunks)],
        hgu_v[...],
        nhot,
    )

    loads[2].wait()
    loads[3].wait()
    loads[6].wait()
    for copy in swaps:
        copy.wait()

    def arrive(buffer, sem):
        pltpu.make_async_remote_copy(
            buffer, buffer, dsp_sem, sem, device_id=partner, device_id_type=MESH
        ).wait_recv()

    def drain(buffer, sem):
        def leave(part):
            pltpu.make_async_remote_copy(
                part, part, sem, inc_sem, device_id=partner, device_id_type=MESH
            ).wait_send()

        leave(buffer.at[pl.ds(0, n - 1)])

        @pl.when(t != h)
        def _():
            leave(buffer.at[n - 1])

    arrive(inc, inc_sem)

    def own(i):
        halves = [
            dot(gather_v[...], inc[pl.ds(hf * side + i * 4, 4)].reshape(big, LANES))
            for hf in range(2)
        ]
        hid_v[i] = hidden(
            [halves[c // chunks][(c % chunks) * 8:(c % chunks + 1) * 8] for c in range(2 * chunks)],
            cgu_v[...],
            2 * ncold,
        )

    loop(n // 8, own)

    def back(i, hf):
        return pltpu.make_async_remote_copy(
            rout.at[hf * side + i], ret.at[row], rout_sem, ret_sem,
            device_id={"rows": 2 * i + h, "heads": hf}, device_id_type=MESH,
        )

    for hf in range(2):
        def down(i):
            o = dot(hid_v[i], cd_v[:, hf * half:(hf + 1) * half])
            o = jnp.concatenate(
                [o[:, c * LANES:(c + 1) * LANES] for c in range(chunks)], axis=0
            ).astype(BF16)
            rout[pl.ds(hf * side + i * 4, 4)] = (
                dot(scatter_v[...], o).astype(BF16).reshape(4, pay, LANES)
            )

        loop(n // 8, down)

        def give(step):
            offset = jnp.where(idx < side // 2, side - 1 - step, step + 1)
            back(lax.rem(idx + offset, side), hf).start()

        loop(side - 1, give)
        here = jnp.logical_and(t == h, h == hf)

        @pl.when(here)
        def _():
            pltpu.make_async_copy(rout.at[hf * side + idx], ret.at[row], ret_sem).start()

        @pl.when(jnp.logical_not(here))
        def _():
            back(idx, hf).start()

    loads[7].wait()

    def hot_down(side):
        part = dot(hot_hidden, hd_v[:, pl.ds(pl.multiple_of(side * half, half), half)])
        return jnp.concatenate(
            [part[:, c * LANES:(c + 1) * LANES] for c in range(chunks)], axis=0
        )

    hot_send[...] = hot_down(other)
    send_hot = pltpu.make_async_remote_copy(
        hot_send, hot_recv, hot_sem.at[0], hot_sem.at[1], device_id=partner, device_id_type=MESH
    )
    send_hot.start()
    result = hot_down(h) + x.astype(F32)

    drain(inc, dsp_sem)
    drain(rout, rout_sem)

    cold_acc[...] = result
    arrive(ret, ret_sem)

    def collect(i):
        cold_acc[...] += dot(
            back_v[i], ret[pl.ds(i * 4 * per, 4 * per)].reshape(4 * per * pay, LANES)
        )

    loop(nb // 4, collect)
    send_hot.wait()
    result = cold_acc[...] + hot_recv[...]
    for c in range(chunks):
        out_ref[:, c * LANES:(c + 1) * LANES] = result[c * REQ:(c + 1) * REQ].astype(out_ref.dtype)


def local(n, residual_in, query, key_cache, value_cache, key_new, value_new, lengths, norm_gain,
          hot_gate, hot_up, hot_down, cold_gate, cold_up, cold_down, active):
    width = hot_gate.shape[1]
    half = width // 2
    chunks = half // LANES
    nb = active.shape[1]
    nhot, ncold = hot_gate.shape[0], cold_gate.shape[0]
    ctx = key_cache.shape[2]
    vmem = pl.BlockSpec(memory_space=pltpu.VMEM)
    hbm = pl.BlockSpec(memory_space=pltpu.HBM)
    pay = CAP * chunks
    dma = pltpu.SemaphoreType.DMA
    return pl.pallas_call(
        functools.partial(kernel, n, nb, ctx, nhot, ncold, width),
        out_shape=pltpu.VMEM(residual_in.shape, residual_in.dtype),
        in_specs=[hbm] * 15,
        out_specs=vmem,
        scratch_shapes=[
            pltpu.VMEM(query.shape, BF16),
            pltpu.VMEM(residual_in.shape, BF16),
            pltpu.VMEM(key_new.shape, BF16),
            pltpu.VMEM(value_new.shape, BF16),
            pltpu.VMEM(norm_gain.shape, BF16),
            pltpu.SMEM(lengths.shape, jnp.int32),
            pltpu.SMEM(active.shape[::-1], jnp.int32),
            pltpu.VMEM((nb // 4, 4 * pay, chunks * REQ), BF16),
            pltpu.VMEM((nb // 4, chunks * REQ, 4 * (n // nb) * pay), BF16),
            pltpu.VMEM((4 * pay, 4 * pay), BF16),
            pltpu.VMEM((4 * pay, 4 * pay), BF16),
            pltpu.VMEM((n // 8, 8, 2 * ncold), BF16),
            pltpu.VMEM(key_cache.shape, BF16),
            pltpu.VMEM(value_cache.shape, BF16),
            pltpu.VMEM((2 * nhot, width), BF16),
            pltpu.VMEM((nhot, width), BF16),
            pltpu.VMEM((4 * ncold, width), BF16),
            pltpu.VMEM((2 * ncold, width), BF16),
            pltpu.VMEM((2, chunks * REQ, LANES), BF16),
            pltpu.VMEM((nb, pay, LANES), BF16),
            pltpu.VMEM((n, pay, LANES), BF16),
            pltpu.VMEM((n, pay, LANES), BF16),
            pltpu.VMEM((n, pay, LANES), BF16),
            pltpu.VMEM((chunks * REQ, LANES), F32),
            pltpu.VMEM((chunks * REQ, LANES), F32),
            pltpu.VMEM((chunks * REQ, LANES), F32),
            dma((15,)), dma((3,)), dma((3,)), dma((2,)), dma((2,)),
            dma(()), dma(()), dma(()), dma(()),
        ],
        compiler_params=pltpu.CompilerParams(
            collective_id=0, has_side_effects=True, vmem_limit_bytes=48 * 1024 * 1024
        ),
        name="decode_step",
    )(*[
        pltpu.with_memory_space_constraint(array, pltpu.HBM)
        for array in (
            query, residual_in, key_new, value_new, norm_gain, lengths, active.T,
            key_cache, value_cache, hot_gate, hot_up, hot_down, cold_gate, cold_up, cold_down,
        )
    ])


def solution(mesh):
    return jax.shard_map(
        functools.partial(local, mesh.shape["rows"]),
        mesh=mesh,
        in_specs=(
            P(("groups", "rows"), "heads"),
            P(("groups", "rows"), "heads"),
            P(("groups", "rows"), "heads", None, None),
            P(("groups", "rows"), "heads", None, None),
            P(("groups", "rows"), "heads", None),
            P(("groups", "rows"), "heads", None),
            P(("groups", "rows")),
            P(),
            P("heads", None),
            P("heads", None),
            P("heads", None),
            P(("rows", "heads"), None),
            P(("rows", "heads"), None),
            P(("rows", "heads"), None),
            P(("groups", "rows"), None),
        ),
        out_specs=P(("groups", "rows"), "heads"),
        check_vma=False,
    )
```

```python
import functools

import jax
import jax.numpy as jnp
from jax import lax
from jax.experimental import pallas as pl
from jax.experimental.pallas import tpu as pltpu
from jax.sharding import PartitionSpec as P

HD = 128
GROUP = 16
CAP = 2
REQ = 8
LANES = 512
F32 = jnp.float32
BF16 = jnp.bfloat16
MESH = pl.DeviceIdType.MESH


def iota(shape, axis):
    return lax.broadcasted_iota(jnp.int32, shape, axis)


def div(v, k):
    return lax.shift_right_logical(v, k.bit_length() - 1) if k & (k - 1) == 0 else lax.div(v, k)


def rem(v, k):
    return v & (k - 1) if k & (k - 1) == 0 else lax.rem(v, k)


def onehot(hit):
    return jnp.where(hit, 1.0, 0.0).astype(BF16)


def dot(a, b):
    return jnp.dot(a, b, preferred_element_type=F32)


def dot_t(a, b):
    return lax.dot_general(a, b, (((1,), (1,)), ((), ())), preferred_element_type=F32)


def loop(count, body):
    if count <= 8:
        for step in range(count):
            body(step)
    else:
        lax.fori_loop(0, count, lambda step, carry: (body(step), carry)[1], 0)


def kernel(n, nb, ctx, nhot, ncold, width, *refs):
    (
        q_hbm, res_hbm, kn_hbm, vn_hbm, gain_hbm, len_hbm, act_hbm,
        kc_hbm, vc_hbm, hg_hbm, hu_hbm, hd_hbm, cg_hbm, cu_hbm, cd_hbm,
        out_ref,
        q_ref, res_ref, kn_ref, vn_ref, gain_ref, len_ref, act_ref,
        sel_v, back_v, gather_v, scatter_v, hid_v,
        kc_v, vc_v, hgu_v, hd_v, cgu_v, cd_v,
        xh, dsp, inc, rout, ret, hot_send, hot_recv, cold_acc,
        load_sem, swap_send, swap_recv, x_sem, hot_sem,
        dsp_sem, inc_sem, rout_sem, ret_sem,
    ) = refs
    half = width // 2
    chunks = half // LANES
    per = n // nb
    row = lax.axis_index("rows")
    h = lax.axis_index("heads")
    other = 1 - h
    t = lax.rem(row, 2)
    idx = lax.div(row, 2)
    partner = {"heads": other}

    loads = [
        (kc_hbm, kc_v),
        (vc_hbm, vc_v),
        (cg_hbm, cgu_v.at[pl.ds(pl.multiple_of(h * ncold, ncold), ncold)]),
        (cu_hbm, cgu_v.at[pl.ds(pl.multiple_of((2 + h) * ncold, ncold), ncold)]),
        (hg_hbm, hgu_v.at[pl.ds(0, nhot)]),
        (hu_hbm, hgu_v.at[pl.ds(nhot, nhot)]),
        (cd_hbm, cd_v.at[pl.ds(pl.multiple_of(h * ncold, ncold), ncold)]),
        (hd_hbm, hd_v),
        (q_hbm, q_ref),
        (kn_hbm, kn_ref),
        (vn_hbm, vn_ref),
        (res_hbm, res_ref),
        (gain_hbm, gain_ref),
        (len_hbm, len_ref),
        (act_hbm, act_ref),
    ]
    loads = [
        pltpu.make_async_copy(src, dst, load_sem.at[i]) for i, (src, dst) in enumerate(loads)
    ]
    for i in (14, 13, 8, 0, 9, 1, 10, 11, 12):
        loads[i].start()

    barrier = pltpu.get_barrier_semaphore()

    def greet(step):
        peer = lax.rem(row + step + 1, n)
        for side in range(2):
            pl.semaphore_signal(
                barrier, inc=1, device_id={"rows": peer, "heads": side}, device_id_type=MESH
            )

    pl.semaphore_signal(barrier, inc=1, device_id=partner, device_id_type=MESH)
    loop(n - 1, greet)

    stack = chunks * REQ
    pay = CAP * chunks
    loads[13].wait()
    loads[14].wait()

    def prepare(i):
        targets = []
        for b in range(4):
            count = jnp.int32(0)
            places = [jnp.int32(-1)] * CAP
            for r in range(REQ):
                on = act_ref[i * 4 + b, r]
                for s in range(CAP):
                    places[s] = jnp.where(
                        jnp.logical_and(on == 1, count == s), jnp.int32(r), places[s]
                    )
                count = count + on
            targets += places
        line = iota((4 * pay, 1), 0)
        target = jnp.full((4 * pay, 1), -1, jnp.int32)
        for k, p in enumerate(targets):
            target = jnp.where(div(line, chunks) == k, p, target)
        target = jnp.where(target < 0, -1, rem(line, chunks) * REQ + target)
        sel_v[i] = onehot(iota((4 * pay, stack), 1) == target)
        column = iota((1, 4 * per * pay), 1)
        slot = div(column, pay * per) * CAP + rem(div(column, chunks), CAP)
        target = jnp.full(column.shape, -1, jnp.int32)
        for k, p in enumerate(targets):
            target = jnp.where(slot == k, p, target)
        target = jnp.where(target < 0, -1, rem(column, chunks) * REQ + target)
        back_v[i] = onehot(iota((stack, 4 * per * pay), 0) == target)

    loop(nb // 4, prepare)

    big = 4 * pay

    def packed(v):
        return rem(v, 8) * chunks + div(v, 8)

    gather_v[...] = onehot(packed(iota((big, 1), 0)) == iota((big, big), 1))
    scatter_v[...] = onehot(packed(iota((1, big), 1)) == iota((big, big), 0))
    for i in (2, 3, 6, 4, 5, 7):
        loads[i].start()

    scale = 1.0 / HD**0.5
    span = REQ * ctx
    rows_q = GROUP * REQ
    col = iota((1, span + HD), 1)
    whose = jnp.where(jnp.logical_and(col >= span, col < span + REQ), col - span, -1)
    for r in range(REQ):
        here = jnp.logical_and(col >= r * ctx, col < r * ctx + len_ref[r])
        whose = jnp.where(here, r, whose)
    mask = rem(iota((rows_q, span + HD), 0), REQ) == whose
    blank = jnp.zeros((HD - REQ, HD), F32)
    ones = jnp.ones((span + HD, HD), BF16)
    for i in (8, 0, 9, 1, 10, 11):
        loads[i].wait()

    pl.semaphore_wait(barrier, 2 * n - 1)

    swaps = [
        (cg_hbm, cgu_v.at[pl.ds(pl.multiple_of(h * ncold, ncold), ncold)]),
        (cu_hbm, cgu_v.at[pl.ds(pl.multiple_of((2 + h) * ncold, ncold), ncold)]),
        (cd_hbm, cd_v.at[pl.ds(pl.multiple_of(h * ncold, ncold), ncold)]),
    ]
    swaps = [
        pltpu.make_async_remote_copy(
            src, dst, swap_send.at[i], swap_recv.at[i], device_id=partner, device_id_type=MESH
        )
        for i, (src, dst) in enumerate(swaps)
    ]
    for copy in swaps:
        copy.start()

    q = q_ref[...].astype(F32)
    kv_local = kc_v.shape[1]
    tiles = []

    def attend(g):
        qs = jnp.concatenate(
            [q[:, (g * GROUP + j) * HD:(g * GROUP + j + 1) * HD] for j in range(GROUP)], axis=0
        )
        key_own = jnp.concatenate([kn_ref[:, g, :].astype(F32), blank], axis=0).astype(BF16)
        keys = jnp.concatenate([kc_v[:, g].reshape(span, HD), key_own], axis=0)
        s = jnp.where(mask, dot_t(qs.astype(BF16), keys) * scale, -1e30)
        e = jnp.exp(s - jnp.max(s, axis=-1, keepdims=True))
        value_own = jnp.concatenate([vn_ref[:, g, :].astype(F32), blank], axis=0).astype(BF16)
        values = jnp.concatenate([vc_v[:, g].reshape(span, HD), value_own], axis=0)
        o = dot(e.astype(BF16), jnp.concatenate([values, ones], axis=1))
        o = o[:, :HD] / o[:, HD:]
        for j in range(GROUP):
            tiles.append(o[j * REQ:(j + 1) * REQ])

    for g in range(kv_local):
        attend(g)

    per_chunk = LANES // HD
    residual = res_ref[...].astype(F32)
    x = jnp.concatenate(
        [
            residual[:, c * LANES:(c + 1) * LANES]
            + jnp.concatenate(tiles[c * per_chunk:(c + 1) * per_chunk], axis=1)
            for c in range(chunks)
        ],
        axis=0,
    ).astype(BF16)
    xh[h] = x

    def select(i):
        dsp[pl.ds(i * 4, 4)] = dot(sel_v[i], x).astype(BF16).reshape(4, pay, LANES)

    loop(nb // 4, select)

    side = n // 2

    def dispatch(step):
        dst = lax.rem(row + step, n)
        return pltpu.make_async_remote_copy(
            dsp.at[lax.div(dst, per)], inc.at[h * side + idx], dsp_sem, inc_sem,
            device_id={"rows": dst, "heads": t}, device_id_type=MESH,
        )

    loop(n - 1, lambda step: dispatch(step + 1).start())

    @pl.when(t == h)
    def _():
        pltpu.make_async_copy(dsp.at[lax.div(row, per)], inc.at[h * side + idx], inc_sem).start()

    @pl.when(t != h)
    def _():
        dispatch(0).start()

    send_x = pltpu.make_async_remote_copy(
        xh.at[h], xh.at[h], x_sem.at[0], x_sem.at[1], device_id=partner, device_id_type=MESH
    )
    send_x.start()
    def hidden(blocks, weights, count):
        total = blocks[0] * blocks[0]
        for block in blocks[1:]:
            total = total + block * block
        rs = lax.rsqrt(jnp.sum(total, axis=-1, keepdims=True) / width + 1e-05)
        normed = jnp.concatenate(
            [
                (
                    block * gain_ref[c * LANES:(c + 1) * LANES].astype(F32)[None, :]
                ).astype(BF16)
                for c, block in enumerate(blocks)
            ],
            axis=1,
        )
        both = dot_t(normed, weights) * rs
        gate, up = both[:, :count], both[:, count:]
        return (gate / (1.0 + jnp.exp(-gate)) * up).astype(BF16)

    loads[4].wait()
    loads[5].wait()
    loads[12].wait()
    send_x.wait()
    whole = [xh[side].astype(F32) for side in range(2)]
    hot_hidden = hidden(
        [whole[c // chunks][(c % chunks) * REQ:(c % chunks + 1) * REQ] for c in range(2 * chunks)],
        hgu_v[...],
        nhot,
    )

    loads[2].wait()
    loads[3].wait()
    loads[6].wait()
    for copy in swaps:
        copy.wait()

    def arrive(buffer, sem):
        pltpu.make_async_remote_copy(
            buffer, buffer, dsp_sem, sem, device_id=partner, device_id_type=MESH
        ).wait_recv()

    def drain(buffer, sem):
        def leave(part):
            pltpu.make_async_remote_copy(
                part, part, sem, inc_sem, device_id=partner, device_id_type=MESH
            ).wait_send()

        leave(buffer.at[pl.ds(0, n - 1)])

        @pl.when(t != h)
        def _():
            leave(buffer.at[n - 1])

    arrive(inc, inc_sem)

    def own(i):
        halves = [
            dot(gather_v[...], inc[pl.ds(hf * side + i * 4, 4)].reshape(big, LANES))
            for hf in range(2)
        ]
        hid_v[i] = hidden(
            [halves[c // chunks][(c % chunks) * 8:(c % chunks + 1) * 8] for c in range(2 * chunks)],
            cgu_v[...],
            2 * ncold,
        )

    loop(n // 8, own)

    def back(i, hf):
        return pltpu.make_async_remote_copy(
            rout.at[hf * side + i], ret.at[row], rout_sem, ret_sem,
            device_id={"rows": 2 * i + h, "heads": hf}, device_id_type=MESH,
        )

    for hf in range(2):
        def down(i):
            o = dot(hid_v[i], cd_v[:, hf * half:(hf + 1) * half])
            o = jnp.concatenate(
                [o[:, c * LANES:(c + 1) * LANES] for c in range(chunks)], axis=0
            ).astype(BF16)
            rout[pl.ds(hf * side + i * 4, 4)] = (
                dot(scatter_v[...], o).astype(BF16).reshape(4, pay, LANES)
            )

        loop(n // 8, down)

        def give(step):
            offset = jnp.where(idx < side // 2, side - 1 - step, step + 1)
            back(lax.rem(idx + offset, side), hf).start()

        loop(side - 1, give)
        here = jnp.logical_and(t == h, h == hf)

        @pl.when(here)
        def _():
            pltpu.make_async_copy(rout.at[hf * side + idx], ret.at[row], ret_sem).start()

        @pl.when(jnp.logical_not(here))
        def _():
            back(idx, hf).start()

    loads[7].wait()

    def hot_down(side):
        part = dot(hot_hidden, hd_v[:, pl.ds(pl.multiple_of(side * half, half), half)])
        return jnp.concatenate(
            [part[:, c * LANES:(c + 1) * LANES] for c in range(chunks)], axis=0
        )

    hot_send[...] = hot_down(other)
    send_hot = pltpu.make_async_remote_copy(
        hot_send, hot_recv, hot_sem.at[0], hot_sem.at[1], device_id=partner, device_id_type=MESH
    )
    send_hot.start()
    result = hot_down(h) + x.astype(F32)

    drain(inc, dsp_sem)
    drain(rout, rout_sem)

    cold_acc[...] = result
    arrive(ret, ret_sem)

    def collect(i):
        cold_acc[...] += dot(
            back_v[i], ret[pl.ds(i * 4 * per, 4 * per)].reshape(4 * per * pay, LANES)
        )

    loop(nb // 4, collect)
    send_hot.wait()
    result = cold_acc[...] + hot_recv[...]
    for c in range(chunks):
        out_ref[:, c * LANES:(c + 1) * LANES] = result[c * REQ:(c + 1) * REQ].astype(out_ref.dtype)


def local(n, residual_in, query, key_cache, value_cache, key_new, value_new, lengths, norm_gain,
          hot_gate, hot_up, hot_down, cold_gate, cold_up, cold_down, active):
    width = hot_gate.shape[1]
    half = width // 2
    chunks = half // LANES
    nb = active.shape[1]
    nhot, ncold = hot_gate.shape[0], cold_gate.shape[0]
    ctx = key_cache.shape[2]
    vmem = pl.BlockSpec(memory_space=pltpu.VMEM)
    hbm = pl.BlockSpec(memory_space=pltpu.HBM)
    pay = CAP * chunks
    dma = pltpu.SemaphoreType.DMA
    return pl.pallas_call(
        functools.partial(kernel, n, nb, ctx, nhot, ncold, width),
        out_shape=pltpu.VMEM(residual_in.shape, residual_in.dtype),
        in_specs=[hbm] * 15,
        out_specs=vmem,
        scratch_shapes=[
            pltpu.VMEM(query.shape, BF16),
            pltpu.VMEM(residual_in.shape, BF16),
            pltpu.VMEM(key_new.shape, BF16),
            pltpu.VMEM(value_new.shape, BF16),
            pltpu.VMEM(norm_gain.shape, BF16),
            pltpu.SMEM(lengths.shape, jnp.int32),
            pltpu.SMEM(active.shape[::-1], jnp.int32),
            pltpu.VMEM((nb // 4, 4 * pay, chunks * REQ), BF16),
            pltpu.VMEM((nb // 4, chunks * REQ, 4 * (n // nb) * pay), BF16),
            pltpu.VMEM((4 * pay, 4 * pay), BF16),
            pltpu.VMEM((4 * pay, 4 * pay), BF16),
            pltpu.VMEM((n // 8, 8, 2 * ncold), BF16),
            pltpu.VMEM(key_cache.shape, BF16),
            pltpu.VMEM(value_cache.shape, BF16),
            pltpu.VMEM((2 * nhot, width), BF16),
            pltpu.VMEM((nhot, width), BF16),
            pltpu.VMEM((4 * ncold, width), BF16),
            pltpu.VMEM((2 * ncold, width), BF16),
            pltpu.VMEM((2, chunks * REQ, LANES), BF16),
            pltpu.VMEM((nb, pay, LANES), BF16),
            pltpu.VMEM((n, pay, LANES), BF16),
            pltpu.VMEM((n, pay, LANES), BF16),
            pltpu.VMEM((n, pay, LANES), BF16),
            pltpu.VMEM((chunks * REQ, LANES), F32),
            pltpu.VMEM((chunks * REQ, LANES), F32),
            pltpu.VMEM((chunks * REQ, LANES), F32),
            dma((15,)), dma((3,)), dma((3,)), dma((2,)), dma((2,)),
            dma(()), dma(()), dma(()), dma(()),
        ],
        compiler_params=pltpu.CompilerParams(
            collective_id=0, has_side_effects=True, vmem_limit_bytes=48 * 1024 * 1024
        ),
        name="decode_step",
    )(*[
        pltpu.with_memory_space_constraint(array, pltpu.HBM)
        for array in (
            query, residual_in, key_new, value_new, norm_gain, lengths, active.T,
            key_cache, value_cache, hot_gate, hot_up, hot_down, cold_gate, cold_up, cold_down,
        )
    ])


def solution(mesh):
    return jax.shard_map(
        functools.partial(local, mesh.shape["rows"]),
        mesh=mesh,
        in_specs=(
            P(("groups", "rows"), "heads"),
            P(("groups", "rows"), "heads"),
            P(("groups", "rows"), "heads", None, None),
            P(("groups", "rows"), "heads", None, None),
            P(("groups", "rows"), "heads", None),
            P(("groups", "rows"), "heads", None),
            P(("groups", "rows")),
            P(),
            P("heads", None),
            P("heads", None),
            P("heads", None),
            P(("rows", "heads"), None),
            P(("rows", "heads"), None),
            P(("rows", "heads"), None),
            P(("groups", "rows"), None),
        ),
        out_specs=P(("groups", "rows"), "heads"),
        check_vma=False,
    )
```

```python
import functools

import jax
import jax.numpy as jnp
from jax import lax
from jax.experimental import pallas as pl
from jax.experimental.pallas import tpu as pltpu
from jax.sharding import PartitionSpec as P

HD = 128
GROUP = 16
CAP = 2
REQ = 8
LANES = 512
F32 = jnp.float32
BF16 = jnp.bfloat16
MESH = pl.DeviceIdType.MESH


def iota(shape, axis):
    return lax.broadcasted_iota(jnp.int32, shape, axis)


def div(v, k):
    return lax.shift_right_logical(v, k.bit_length() - 1) if k & (k - 1) == 0 else lax.div(v, k)


def rem(v, k):
    return v & (k - 1) if k & (k - 1) == 0 else lax.rem(v, k)


def onehot(hit):
    return jnp.where(hit, 1.0, 0.0).astype(BF16)


def dot(a, b):
    return jnp.dot(a, b, preferred_element_type=F32)


def dot_t(a, b):
    return lax.dot_general(a, b, (((1,), (1,)), ((), ())), preferred_element_type=F32)


def loop(count, body):
    if count <= 8:
        for step in range(count):
            body(step)
    else:
        lax.fori_loop(0, count, lambda step, carry: (body(step), carry)[1], 0)


def kernel(n, nb, ctx, nhot, ncold, width, *refs):
    (
        q_hbm, res_hbm, kn_hbm, vn_hbm, gain_hbm, len_hbm, act_hbm,
        kc_hbm, vc_hbm, hg_hbm, hu_hbm, hd_hbm, cg_hbm, cu_hbm, cd_hbm,
        out_ref,
        q_ref, res_ref, kn_ref, vn_ref, gain_ref, len_ref, act_ref,
        sel_v, back_v, gather_v, scatter_v, hid_v,
        kc_v, vc_v, hgu_v, hd_v, cgu_v, cd_v,
        xh, dsp, inc, rout, ret, hot_send, hot_recv, cold_acc,
        load_sem, swap_send, swap_recv, x_sem, hot_sem,
        dsp_sem, inc_sem, rout_sem, ret_sem,
    ) = refs
    half = width // 2
    chunks = half // LANES
    per = n // nb
    row = lax.axis_index("rows")
    h = lax.axis_index("heads")
    other = 1 - h
    t = lax.rem(row, 2)
    idx = lax.div(row, 2)
    partner = {"heads": other}

    loads = [
        (kc_hbm, kc_v),
        (vc_hbm, vc_v),
        (cg_hbm, cgu_v.at[pl.ds(pl.multiple_of(h * ncold, ncold), ncold)]),
        (cu_hbm, cgu_v.at[pl.ds(pl.multiple_of((2 + h) * ncold, ncold), ncold)]),
        (hg_hbm, hgu_v.at[pl.ds(0, nhot)]),
        (hu_hbm, hgu_v.at[pl.ds(nhot, nhot)]),
        (cd_hbm, cd_v.at[pl.ds(pl.multiple_of(h * ncold, ncold), ncold)]),
        (hd_hbm, hd_v),
        (q_hbm, q_ref),
        (kn_hbm, kn_ref),
        (vn_hbm, vn_ref),
        (res_hbm, res_ref),
        (gain_hbm, gain_ref),
        (len_hbm, len_ref),
        (act_hbm, act_ref),
    ]
    loads = [
        pltpu.make_async_copy(src, dst, load_sem.at[i]) for i, (src, dst) in enumerate(loads)
    ]
    for i in (14, 13, 8, 0, 9, 1, 10, 11, 12):
        loads[i].start()

    barrier = pltpu.get_barrier_semaphore()

    def greet(step):
        peer = lax.rem(row + step + 1, n)
        for side in range(2):
            pl.semaphore_signal(
                barrier, inc=1, device_id={"rows": peer, "heads": side}, device_id_type=MESH
            )

    pl.semaphore_signal(barrier, inc=1, device_id=partner, device_id_type=MESH)
    loop(n - 1, greet)

    stack = chunks * REQ
    pay = CAP * chunks
    loads[13].wait()
    loads[14].wait()

    def prepare(i):
        targets = []
        for b in range(4):
            count = jnp.int32(0)
            places = [jnp.int32(-1)] * CAP
            for r in range(REQ):
                on = act_ref[i * 4 + b, r]
                for s in range(CAP):
                    places[s] = jnp.where(
                        jnp.logical_and(on == 1, count == s), jnp.int32(r), places[s]
                    )
                count = count + on
            targets += places
        line = iota((4 * pay, 1), 0)
        target = jnp.full((4 * pay, 1), -1, jnp.int32)
        for k, p in enumerate(targets):
            target = jnp.where(div(line, chunks) == k, p, target)
        target = jnp.where(target < 0, -1, rem(line, chunks) * REQ + target)
        sel_v[i] = onehot(iota((4 * pay, stack), 1) == target)
        column = iota((1, 4 * per * pay), 1)
        slot = div(column, pay * per) * CAP + rem(div(column, chunks), CAP)
        target = jnp.full(column.shape, -1, jnp.int32)
        for k, p in enumerate(targets):
            target = jnp.where(slot == k, p, target)
        target = jnp.where(target < 0, -1, rem(column, chunks) * REQ + target)
        back_v[i] = onehot(iota((stack, 4 * per * pay), 0) == target)

    loop(nb // 4, prepare)

    big = 4 * pay

    def packed(v):
        return rem(v, 8) * chunks + div(v, 8)

    gather_v[...] = onehot(packed(iota((big, 1), 0)) == iota((big, big), 1))
    scatter_v[...] = onehot(packed(iota((1, big), 1)) == iota((big, big), 0))
    for i in (2, 3, 6, 4, 5, 7):
        loads[i].start()

    scale = 1.0 / HD**0.5
    span = REQ * ctx
    rows_q = GROUP * REQ
    col = iota((1, span + HD), 1)
    whose = jnp.where(jnp.logical_and(col >= span, col < span + REQ), col - span, -1)
    for r in range(REQ):
        here = jnp.logical_and(col >= r * ctx, col < r * ctx + len_ref[r])
        whose = jnp.where(here, r, whose)
    mask = rem(iota((rows_q, span + HD), 0), REQ) == whose
    blank = jnp.zeros((HD - REQ, HD), F32)
    ones = jnp.ones((span + HD, HD), BF16)
    for i in (8, 0, 9, 1, 10, 11):
        loads[i].wait()

    q = q_ref[...].astype(F32)
    kv_local = kc_v.shape[1]
    tiles = []

    def attend(g):
        qs = jnp.concatenate(
            [q[:, (g * GROUP + j) * HD:(g * GROUP + j + 1) * HD] for j in range(GROUP)], axis=0
        )
        key_own = jnp.concatenate([kn_ref[:, g, :].astype(F32), blank], axis=0).astype(BF16)
        keys = jnp.concatenate([kc_v[:, g].reshape(span, HD), key_own], axis=0)
        s = jnp.where(mask, dot_t(qs.astype(BF16), keys) * scale, -1e30)
        e = jnp.exp(s - jnp.max(s, axis=-1, keepdims=True))
        value_own = jnp.concatenate([vn_ref[:, g, :].astype(F32), blank], axis=0).astype(BF16)
        values = jnp.concatenate([vc_v[:, g].reshape(span, HD), value_own], axis=0)
        o = dot(e.astype(BF16), jnp.concatenate([values, ones], axis=1))
        o = o[:, :HD] / o[:, HD:]
        for j in range(GROUP):
            tiles.append(o[j * REQ:(j + 1) * REQ])

    for g in range(kv_local):
        attend(g)

    per_chunk = LANES // HD
    residual = res_ref[...].astype(F32)
    x = jnp.concatenate(
        [
            residual[:, c * LANES:(c + 1) * LANES]
            + jnp.concatenate(tiles[c * per_chunk:(c + 1) * per_chunk], axis=1)
            for c in range(chunks)
        ],
        axis=0,
    ).astype(BF16)
    xh[h] = x

    def select(i):
        dsp[pl.ds(i * 4, 4)] = dot(sel_v[i], x).astype(BF16).reshape(4, pay, LANES)

    loop(nb // 4, select)

    pl.semaphore_wait(barrier, 2 * n - 1)

    side = n // 2

    def dispatch(step):
        dst = lax.rem(row + step, n)
        return pltpu.make_async_remote_copy(
            dsp.at[lax.div(dst, per)], inc.at[h * side + idx], dsp_sem, inc_sem,
            device_id={"rows": dst, "heads": t}, device_id_type=MESH,
        )

    loop(n - 1, lambda step: dispatch(step + 1).start())

    @pl.when(t == h)
    def _():
        pltpu.make_async_copy(dsp.at[lax.div(row, per)], inc.at[h * side + idx], inc_sem).start()

    @pl.when(t != h)
    def _():
        dispatch(0).start()

    send_x = pltpu.make_async_remote_copy(
        xh.at[h], xh.at[h], x_sem.at[0], x_sem.at[1], device_id=partner, device_id_type=MESH
    )
    send_x.start()
    swaps = [
        (cg_hbm, cgu_v.at[pl.ds(pl.multiple_of(h * ncold, ncold), ncold)]),
        (cu_hbm, cgu_v.at[pl.ds(pl.multiple_of((2 + h) * ncold, ncold), ncold)]),
        (cd_hbm, cd_v.at[pl.ds(pl.multiple_of(h * ncold, ncold), ncold)]),
    ]
    swaps = [
        pltpu.make_async_remote_copy(
            src, dst, swap_send.at[i], swap_recv.at[i], device_id=partner, device_id_type=MESH
        )
        for i, (src, dst) in enumerate(swaps)
    ]
    for copy in swaps:
        copy.start()

    def hidden(blocks, weights, count):
        total = blocks[0] * blocks[0]
        for block in blocks[1:]:
            total = total + block * block
        rs = lax.rsqrt(jnp.sum(total, axis=-1, keepdims=True) / width + 1e-05)
        normed = jnp.concatenate(
            [
                (
                    block * gain_ref[c * LANES:(c + 1) * LANES].astype(F32)[None, :]
                ).astype(BF16)
                for c, block in enumerate(blocks)
            ],
            axis=1,
        )
        both = dot_t(weights, normed).T * rs
        gate, up = both[:, :count], both[:, count:]
        return (gate / (1.0 + jnp.exp(-gate)) * up).astype(BF16)

    loads[4].wait()
    loads[5].wait()
    loads[12].wait()
    send_x.wait()
    whole = [xh[side].astype(F32) for side in range(2)]
    hot_hidden = hidden(
        [whole[c // chunks][(c % chunks) * REQ:(c % chunks + 1) * REQ] for c in range(2 * chunks)],
        hgu_v[...],
        nhot,
    )

    loads[2].wait()
    loads[3].wait()
    loads[6].wait()
    for copy in swaps:
        copy.wait()

    def arrive(buffer, sem):
        pltpu.make_async_remote_copy(
            buffer, buffer, dsp_sem, sem, device_id=partner, device_id_type=MESH
        ).wait_recv()

    def drain(buffer, sem):
        def leave(part):
            pltpu.make_async_remote_copy(
                part, part, sem, inc_sem, device_id=partner, device_id_type=MESH
            ).wait_send()

        leave(buffer.at[pl.ds(0, n - 1)])

        @pl.when(t != h)
        def _():
            leave(buffer.at[n - 1])

    arrive(inc, inc_sem)

    def own(i):
        halves = [
            dot(gather_v[...], inc[pl.ds(hf * side + i * 4, 4)].reshape(big, LANES))
            for hf in range(2)
        ]
        hid_v[i] = hidden(
            [halves[c // chunks][(c % chunks) * 8:(c % chunks + 1) * 8] for c in range(2 * chunks)],
            cgu_v[...],
            2 * ncold,
        )

    loop(n // 8, own)

    def back(i, hf):
        return pltpu.make_async_remote_copy(
            rout.at[hf * side + i], ret.at[row], rout_sem, ret_sem,
            device_id={"rows": 2 * i + h, "heads": hf}, device_id_type=MESH,
        )

    for hf in range(2):
        def down(i):
            o = dot(hid_v[i], cd_v[:, hf * half:(hf + 1) * half])
            o = jnp.concatenate(
                [o[:, c * LANES:(c + 1) * LANES] for c in range(chunks)], axis=0
            ).astype(BF16)
            rout[pl.ds(hf * side + i * 4, 4)] = (
                dot(scatter_v[...], o).astype(BF16).reshape(4, pay, LANES)
            )

        loop(n // 8, down)

        def give(step):
            offset = jnp.where(idx < side // 2, side - 1 - step, step + 1)
            back(lax.rem(idx + offset, side), hf).start()

        loop(side - 1, give)
        here = jnp.logical_and(t == h, h == hf)

        @pl.when(here)
        def _():
            pltpu.make_async_copy(rout.at[hf * side + idx], ret.at[row], ret_sem).start()

        @pl.when(jnp.logical_not(here))
        def _():
            back(idx, hf).start()

    loads[7].wait()

    def hot_down(side):
        part = dot(hot_hidden, hd_v[:, pl.ds(pl.multiple_of(side * half, half), half)])
        return jnp.concatenate(
            [part[:, c * LANES:(c + 1) * LANES] for c in range(chunks)], axis=0
        )

    hot_send[...] = hot_down(other)
    send_hot = pltpu.make_async_remote_copy(
        hot_send, hot_recv, hot_sem.at[0], hot_sem.at[1], device_id=partner, device_id_type=MESH
    )
    send_hot.start()
    result = hot_down(h) + x.astype(F32)

    drain(inc, dsp_sem)
    drain(rout, rout_sem)

    cold_acc[...] = result
    arrive(ret, ret_sem)

    def collect(i):
        cold_acc[...] += dot(
            back_v[i], ret[pl.ds(i * 4 * per, 4 * per)].reshape(4 * per * pay, LANES)
        )

    loop(nb // 4, collect)
    send_hot.wait()
    result = cold_acc[...] + hot_recv[...]
    for c in range(chunks):
        out_ref[:, c * LANES:(c + 1) * LANES] = result[c * REQ:(c + 1) * REQ].astype(out_ref.dtype)


def local(n, residual_in, query, key_cache, value_cache, key_new, value_new, lengths, norm_gain,
          hot_gate, hot_up, hot_down, cold_gate, cold_up, cold_down, active):
    width = hot_gate.shape[1]
    half = width // 2
    chunks = half // LANES
    nb = active.shape[1]
    nhot, ncold = hot_gate.shape[0], cold_gate.shape[0]
    ctx = key_cache.shape[2]
    vmem = pl.BlockSpec(memory_space=pltpu.VMEM)
    hbm = pl.BlockSpec(memory_space=pltpu.HBM)
    pay = CAP * chunks
    dma = pltpu.SemaphoreType.DMA
    return pl.pallas_call(
        functools.partial(kernel, n, nb, ctx, nhot, ncold, width),
        out_shape=pltpu.VMEM(residual_in.shape, residual_in.dtype),
        in_specs=[hbm] * 15,
        out_specs=vmem,
        scratch_shapes=[
            pltpu.VMEM(query.shape, BF16),
            pltpu.VMEM(residual_in.shape, BF16),
            pltpu.VMEM(key_new.shape, BF16),
            pltpu.VMEM(value_new.shape, BF16),
            pltpu.VMEM(norm_gain.shape, BF16),
            pltpu.SMEM(lengths.shape, jnp.int32),
            pltpu.SMEM(active.shape[::-1], jnp.int32),
            pltpu.VMEM((nb // 4, 4 * pay, chunks * REQ), BF16),
            pltpu.VMEM((nb // 4, chunks * REQ, 4 * (n // nb) * pay), BF16),
            pltpu.VMEM((4 * pay, 4 * pay), BF16),
            pltpu.VMEM((4 * pay, 4 * pay), BF16),
            pltpu.VMEM((n // 8, 8, 2 * ncold), BF16),
            pltpu.VMEM(key_cache.shape, BF16),
            pltpu.VMEM(value_cache.shape, BF16),
            pltpu.VMEM((2 * nhot, width), BF16),
            pltpu.VMEM((nhot, width), BF16),
            pltpu.VMEM((4 * ncold, width), BF16),
            pltpu.VMEM((2 * ncold, width), BF16),
            pltpu.VMEM((2, chunks * REQ, LANES), BF16),
            pltpu.VMEM((nb, pay, LANES), BF16),
            pltpu.VMEM((n, pay, LANES), BF16),
            pltpu.VMEM((n, pay, LANES), BF16),
            pltpu.VMEM((n, pay, LANES), BF16),
            pltpu.VMEM((chunks * REQ, LANES), F32),
            pltpu.VMEM((chunks * REQ, LANES), F32),
            pltpu.VMEM((chunks * REQ, LANES), F32),
            dma((15,)), dma((3,)), dma((3,)), dma((2,)), dma((2,)),
            dma(()), dma(()), dma(()), dma(()),
        ],
        compiler_params=pltpu.CompilerParams(
            collective_id=0, has_side_effects=True, vmem_limit_bytes=48 * 1024 * 1024
        ),
        name="decode_step",
    )(*[
        pltpu.with_memory_space_constraint(array, pltpu.HBM)
        for array in (
            query, residual_in, key_new, value_new, norm_gain, lengths, active.T,
            key_cache, value_cache, hot_gate, hot_up, hot_down, cold_gate, cold_up, cold_down,
        )
    ])


def solution(mesh):
    return jax.shard_map(
        functools.partial(local, mesh.shape["rows"]),
        mesh=mesh,
        in_specs=(
            P(("groups", "rows"), "heads"),
            P(("groups", "rows"), "heads"),
            P(("groups", "rows"), "heads", None, None),
            P(("groups", "rows"), "heads", None, None),
            P(("groups", "rows"), "heads", None),
            P(("groups", "rows"), "heads", None),
            P(("groups", "rows")),
            P(),
            P("heads", None),
            P("heads", None),
            P("heads", None),
            P(("rows", "heads"), None),
            P(("rows", "heads"), None),
            P(("rows", "heads"), None),
            P(("groups", "rows"), None),
        ),
        out_specs=P(("groups", "rows"), "heads"),
        check_vma=False,
    )
```

```python
import functools

import jax
import jax.numpy as jnp
from jax import lax
from jax.experimental import pallas as pl
from jax.experimental.pallas import tpu as pltpu
from jax.sharding import PartitionSpec as P

HD = 128
GROUP = 16
CAP = 2
REQ = 8
LANES = 512
F32 = jnp.float32
BF16 = jnp.bfloat16
MESH = pl.DeviceIdType.MESH


def iota(shape, axis):
    return lax.broadcasted_iota(jnp.int32, shape, axis)


def div(v, k):
    return lax.shift_right_logical(v, k.bit_length() - 1) if k & (k - 1) == 0 else lax.div(v, k)


def rem(v, k):
    return v & (k - 1) if k & (k - 1) == 0 else lax.rem(v, k)


def onehot(hit):
    return jnp.where(hit, 1.0, 0.0).astype(BF16)


def dot(a, b):
    return jnp.dot(a, b, preferred_element_type=F32)


def dot_t(a, b):
    return lax.dot_general(a, b, (((1,), (1,)), ((), ())), preferred_element_type=F32)


def loop(count, body):
    if count <= 8:
        for step in range(count):
            body(step)
    else:
        lax.fori_loop(0, count, lambda step, carry: (body(step), carry)[1], 0)


def kernel(n, nb, ctx, nhot, ncold, width, *refs):
    (
        q_hbm, res_hbm, kn_hbm, vn_hbm, gain_hbm, len_hbm, act_hbm,
        kc_hbm, vc_hbm, hg_hbm, hu_hbm, hd_hbm, cg_hbm, cu_hbm, cd_hbm,
        out_ref,
        q_ref, res_ref, kn_ref, vn_ref, gain_ref, len_ref, act_ref,
        sel_v, back_v, turn_v, hid_v,
        kc_v, vc_v, hgu_v, hd_v, cgu_v, cd_v,
        xh, dsp, inc, rout, ret, hot_send, hot_recv, cold_acc,
        load_sem, swap_send, swap_recv, x_sem, hot_sem,
        dsp_sem, inc_sem, rout_sem, ret_sem,
    ) = refs
    half = width // 2
    chunks = half // LANES
    per = n // nb
    row = lax.axis_index("rows")
    h = lax.axis_index("heads")
    other = 1 - h
    t = lax.rem(row, 2)
    idx = lax.div(row, 2)
    partner = {"heads": other}

    barrier = pltpu.get_barrier_semaphore()

    def greet(peer, core):
        pl.semaphore_signal(
            barrier, inc=1, device_id={"rows": peer, "heads": core}, device_id_type=MESH
        )

    loop(n - 1, lambda step: greet(lax.rem(row + step + 1, n), t))
    pl.semaphore_signal(barrier, inc=1, device_id=partner, device_id_type=MESH)

    @pl.when(t == h)
    def _():
        loop(n // 2 - 1, lambda step: greet(lax.rem(row + 2 * step + 2, n), 1 - t))

    @pl.when(t != h)
    def _():
        loop(n // 2, lambda step: greet(lax.rem(row + 2 * step + 1, n), 1 - t))

    loads = [
        (kc_hbm, kc_v),
        (vc_hbm, vc_v),
        (cg_hbm, cgu_v.at[pl.ds(pl.multiple_of(h * ncold, ncold), ncold)]),
        (cu_hbm, cgu_v.at[pl.ds(pl.multiple_of((2 + h) * ncold, ncold), ncold)]),
        (hg_hbm, hgu_v.at[pl.ds(0, nhot)]),
        (hu_hbm, hgu_v.at[pl.ds(nhot, nhot)]),
        (cd_hbm, cd_v.at[pl.ds(pl.multiple_of(h * ncold, ncold), ncold)]),
        (hd_hbm, hd_v),
        (q_hbm, q_ref),
        (kn_hbm, kn_ref),
        (vn_hbm, vn_ref),
        (res_hbm, res_ref),
        (gain_hbm, gain_ref),
        (len_hbm, len_ref),
        (act_hbm, act_ref),
    ]
    loads = [
        pltpu.make_async_copy(src, dst, load_sem.at[i]) for i, (src, dst) in enumerate(loads)
    ]
    for i in (14, 13, 8, 0, 9, 1, 10, 11, 12):
        loads[i].start()

    stack = chunks * REQ
    pay = CAP * chunks
    loads[13].wait()
    loads[14].wait()

    def slots(i):
        targets = []
        for b in range(4):
            count = jnp.int32(0)
            places = [jnp.int32(-1)] * CAP
            for r in range(REQ):
                on = act_ref[i * 4 + b, r]
                for s in range(CAP):
                    places[s] = jnp.where(
                        jnp.logical_and(on == 1, count == s), jnp.int32(r), places[s]
                    )
                count = count + on
            targets += places
        return targets

    def prepare(i):
        line = iota((4 * pay, 1), 0)
        target = jnp.full((4 * pay, 1), -1, jnp.int32)
        for k, p in enumerate(slots(i)):
            target = jnp.where(div(line, chunks) == k, p, target)
        target = jnp.where(target < 0, -1, rem(line, chunks) * REQ + target)
        sel_v[i] = onehot(iota((4 * pay, stack), 1) == target)
    loop(nb // 4, prepare)
    for i in (2, 3, 6, 4, 5, 7):
        loads[i].start()

    scale = 1.0 / HD**0.5
    span = REQ * ctx
    rows_q = GROUP * REQ
    col = iota((1, span + HD), 1)
    whose = jnp.where(jnp.logical_and(col >= span, col < span + REQ), col - span, -1)
    for r in range(REQ):
        here = jnp.logical_and(col >= r * ctx, col < r * ctx + len_ref[r])
        whose = jnp.where(here, r, whose)
    mask = rem(iota((rows_q, span + HD), 0), REQ) == whose
    blank = jnp.zeros((HD - REQ, HD), F32)
    ones = jnp.ones((span + HD, HD), BF16)
    for i in (8, 0, 9, 1, 10, 11):
        loads[i].wait()

    q = q_ref[...].astype(F32)
    kv_local = kc_v.shape[1]
    tiles = []

    def attend(g):
        qs = jnp.concatenate(
            [q[:, (g * GROUP + j) * HD:(g * GROUP + j + 1) * HD] for j in range(GROUP)], axis=0
        )
        key_own = jnp.concatenate([kn_ref[:, g, :].astype(F32), blank], axis=0).astype(BF16)
        keys = jnp.concatenate([kc_v[:, g].reshape(span, HD), key_own], axis=0)
        s = jnp.where(mask, dot_t(qs.astype(BF16), keys) * scale, -1e30)
        e = jnp.exp(s - jnp.max(s, axis=-1, keepdims=True))
        value_own = jnp.concatenate([vn_ref[:, g, :].astype(F32), blank], axis=0).astype(BF16)
        values = jnp.concatenate([vc_v[:, g].reshape(span, HD), value_own], axis=0)
        o = dot(e.astype(BF16), jnp.concatenate([values, ones], axis=1))
        o = o[:, :HD] / o[:, HD:]
        for j in range(GROUP):
            tiles.append(o[j * REQ:(j + 1) * REQ])

    for g in range(kv_local):
        attend(g)

    per_chunk = LANES // HD
    residual = res_ref[...].astype(F32)
    x = jnp.concatenate(
        [
            residual[:, c * LANES:(c + 1) * LANES]
            + jnp.concatenate(tiles[c * per_chunk:(c + 1) * per_chunk], axis=1)
            for c in range(chunks)
        ],
        axis=0,
    ).astype(BF16)
    xh[h] = x

    def select(i):
        dsp[pl.ds(i * 4, 4)] = dot(sel_v[i], x).astype(BF16).reshape(4, pay, LANES)

    loop(nb // 4, select)

    pl.semaphore_wait(barrier, n + n // 2 - jnp.where(t == h, 1, 0))

    side = n // 2

    def dispatch(step):
        dst = lax.rem(row + step, n)
        return pltpu.make_async_remote_copy(
            dsp.at[lax.div(dst, per)], inc.at[h * side + idx], dsp_sem, inc_sem,
            device_id={"rows": dst, "heads": t}, device_id_type=MESH,
        )

    loop(n - 1, lambda step: dispatch(step + 1).start())

    @pl.when(t == h)
    def _():
        pltpu.make_async_copy(dsp.at[lax.div(row, per)], inc.at[h * side + idx], inc_sem).start()

    @pl.when(t != h)
    def _():
        dispatch(0).start()

    send_x = pltpu.make_async_remote_copy(
        xh.at[h], xh.at[h], x_sem.at[0], x_sem.at[1], device_id=partner, device_id_type=MESH
    )
    send_x.start()
    swaps = [
        (cg_hbm, cgu_v.at[pl.ds(pl.multiple_of(h * ncold, ncold), ncold)]),
        (cu_hbm, cgu_v.at[pl.ds(pl.multiple_of((2 + h) * ncold, ncold), ncold)]),
        (cd_hbm, cd_v.at[pl.ds(pl.multiple_of(h * ncold, ncold), ncold)]),
    ]
    swaps = [
        pltpu.make_async_remote_copy(
            src, dst, swap_send.at[i], swap_recv.at[i], device_id=partner, device_id_type=MESH
        )
        for i, (src, dst) in enumerate(swaps)
    ]
    for copy in swaps:
        copy.start()

    def prepare_back(i):
        column = iota((1, 4 * per * pay), 1)
        slot = div(column, pay * per) * CAP + rem(div(column, chunks), CAP)
        target = jnp.full(column.shape, -1, jnp.int32)
        for k, p in enumerate(slots(i)):
            target = jnp.where(slot == k, p, target)
        target = jnp.where(target < 0, -1, rem(column, chunks) * REQ + target)
        back_v[i] = onehot(iota((stack, 4 * per * pay), 0) == target)

    loop(nb // 4, prepare_back)

    def hidden(blocks, weights, count):
        total = blocks[0] * blocks[0]
        for block in blocks[1:]:
            total = total + block * block
        rs = lax.rsqrt(jnp.sum(total, axis=-1, keepdims=True) / width + 1e-05)
        normed = jnp.concatenate(
            [
                (
                    block * gain_ref[c * LANES:(c + 1) * LANES].astype(F32)[None, :]
                ).astype(BF16)
                for c, block in enumerate(blocks)
            ],
            axis=1,
        )
        both = dot_t(normed, weights) * rs
        gate, up = both[:, :count], both[:, count:]
        return (gate / (1.0 + jnp.exp(-gate)) * up).astype(BF16)

    loads[4].wait()
    loads[5].wait()
    loads[12].wait()
    send_x.wait()
    whole = [xh[side].astype(F32) for side in range(2)]
    hot_hidden = hidden(
        [whole[c // chunks][(c % chunks) * REQ:(c % chunks + 1) * REQ] for c in range(2 * chunks)],
        hgu_v[...],
        nhot,
    )

    loads[2].wait()
    loads[3].wait()
    loads[6].wait()
    for copy in swaps:
        copy.wait()

    def arrive(buffer, sem):
        pltpu.make_async_remote_copy(
            buffer, buffer, dsp_sem, sem, device_id=partner, device_id_type=MESH
        ).wait_recv()

    def drain(buffer, sem):
        def leave(part):
            pltpu.make_async_remote_copy(
                part, part, sem, inc_sem, device_id=partner, device_id_type=MESH
            ).wait_send()

        leave(buffer.at[pl.ds(0, n - 1)])

        @pl.when(t != h)
        def _():
            leave(buffer.at[n - 1])

    big = 4 * pay
    arrive(inc, inc_sem)

    def own(i):
        for hf in range(2):
            came = inc[pl.ds(hf * side + i * 4, 4)].reshape(big, LANES).astype(F32)
            for l in range(per_chunk):
                turn_v[hf, l] = came[:, l * HD:(l + 1) * HD]
        hid_v[i] = hidden(
            [
                jnp.concatenate(
                    [
                        turn_v[c // chunks, l, pl.ds(c % chunks, 8, stride=chunks)]
                        for l in range(per_chunk)
                    ],
                    axis=1,
                )
                for c in range(2 * chunks)
            ],
            cgu_v[...],
            2 * ncold,
        )

    loop(n // 8, own)

    def back(i, hf):
        return pltpu.make_async_remote_copy(
            rout.at[hf * side + i], ret.at[row], rout_sem, ret_sem,
            device_id={"rows": 2 * i + h, "heads": hf}, device_id_type=MESH,
        )

    for hf in range(2):
        def down(i):
            o = dot(hid_v[i], cd_v[:, hf * half:(hf + 1) * half])
            for c in range(chunks):
                for l in range(per_chunk):
                    turn_v[hf, l, pl.ds(c, 8, stride=chunks)] = (
                        o[:, c * LANES + l * HD:c * LANES + (l + 1) * HD]
                    )
            turned = jnp.concatenate([turn_v[hf, l] for l in range(per_chunk)], axis=1)
            rout[pl.ds(hf * side + i * 4, 4)] = turned.astype(BF16).reshape(4, pay, LANES)

        loop(n // 8, down)

        def give(step):
            offset = jnp.where(idx < side // 2, side - 1 - step, step + 1)
            back(lax.rem(idx + offset, side), hf).start()

        loop(side - 1, give)
        here = jnp.logical_and(t == h, h == hf)

        @pl.when(here)
        def _():
            pltpu.make_async_copy(rout.at[hf * side + idx], ret.at[row], ret_sem).start()

        @pl.when(jnp.logical_not(here))
        def _():
            back(idx, hf).start()

    loads[7].wait()

    def hot_down(side):
        part = dot(hot_hidden, hd_v[:, pl.ds(pl.multiple_of(side * half, half), half)])
        return jnp.concatenate(
            [part[:, c * LANES:(c + 1) * LANES] for c in range(chunks)], axis=0
        )

    hot_send[...] = hot_down(other)
    send_hot = pltpu.make_async_remote_copy(
        hot_send, hot_recv, hot_sem.at[0], hot_sem.at[1], device_id=partner, device_id_type=MESH
    )
    send_hot.start()
    result = hot_down(h) + x.astype(F32)

    drain(inc, dsp_sem)
    drain(rout, rout_sem)

    cold_acc[...] = result
    arrive(ret, ret_sem)

    def collect(i):
        cold_acc[...] += dot(
            back_v[i], ret[pl.ds(i * 4 * per, 4 * per)].reshape(4 * per * pay, LANES)
        )

    loop(nb // 4, collect)
    send_hot.wait()
    result = cold_acc[...] + hot_recv[...]
    for c in range(chunks):
        out_ref[:, c * LANES:(c + 1) * LANES] = result[c * REQ:(c + 1) * REQ].astype(out_ref.dtype)


def local(n, residual_in, query, key_cache, value_cache, key_new, value_new, lengths, norm_gain,
          hot_gate, hot_up, hot_down, cold_gate, cold_up, cold_down, active):
    width = hot_gate.shape[1]
    half = width // 2
    chunks = half // LANES
    nb = active.shape[1]
    nhot, ncold = hot_gate.shape[0], cold_gate.shape[0]
    ctx = key_cache.shape[2]
    vmem = pl.BlockSpec(memory_space=pltpu.VMEM)
    hbm = pl.BlockSpec(memory_space=pltpu.HBM)
    pay = CAP * chunks
    dma = pltpu.SemaphoreType.DMA
    return pl.pallas_call(
        functools.partial(kernel, n, nb, ctx, nhot, ncold, width),
        out_shape=pltpu.VMEM(residual_in.shape, residual_in.dtype),
        in_specs=[hbm] * 15,
        out_specs=vmem,
        scratch_shapes=[
            pltpu.VMEM(query.shape, BF16),
            pltpu.VMEM(residual_in.shape, BF16),
            pltpu.VMEM(key_new.shape, BF16),
            pltpu.VMEM(value_new.shape, BF16),
            pltpu.VMEM(norm_gain.shape, BF16),
            pltpu.SMEM(lengths.shape, jnp.int32),
            pltpu.SMEM(active.shape[::-1], jnp.int32),
            pltpu.VMEM((nb // 4, 4 * pay, chunks * REQ), BF16),
            pltpu.VMEM((nb // 4, chunks * REQ, 4 * (n // nb) * pay), BF16),
            pltpu.VMEM((2, LANES // HD, 4 * pay, HD), F32),
            pltpu.VMEM((n // 8, 8, 2 * ncold), BF16),
            pltpu.VMEM(key_cache.shape, BF16),
            pltpu.VMEM(value_cache.shape, BF16),
            pltpu.VMEM((2 * nhot, width), BF16),
            pltpu.VMEM((nhot, width), BF16),
            pltpu.VMEM((4 * ncold, width), BF16),
            pltpu.VMEM((2 * ncold, width), BF16),
            pltpu.VMEM((2, chunks * REQ, LANES), BF16),
            pltpu.VMEM((nb, pay, LANES), BF16),
            pltpu.VMEM((n, pay, LANES), BF16),
            pltpu.VMEM((n, pay, LANES), BF16),
            pltpu.VMEM((n, pay, LANES), BF16),
            pltpu.VMEM((chunks * REQ, LANES), F32),
            pltpu.VMEM((chunks * REQ, LANES), F32),
            pltpu.VMEM((chunks * REQ, LANES), F32),
            dma((15,)), dma((3,)), dma((3,)), dma((2,)), dma((2,)),
            dma(()), dma(()), dma(()), dma(()),
        ],
        compiler_params=pltpu.CompilerParams(
            collective_id=0, has_side_effects=True, vmem_limit_bytes=48 * 1024 * 1024
        ),
        name="decode_step",
    )(*[
        pltpu.with_memory_space_constraint(array, pltpu.HBM)
        for array in (
            query, residual_in, key_new, value_new, norm_gain, lengths, active.T,
            key_cache, value_cache, hot_gate, hot_up, hot_down, cold_gate, cold_up, cold_down,
        )
    ])


def solution(mesh):
    return jax.shard_map(
        functools.partial(local, mesh.shape["rows"]),
        mesh=mesh,
        in_specs=(
            P(("groups", "rows"), "heads"),
            P(("groups", "rows"), "heads"),
            P(("groups", "rows"), "heads", None, None),
            P(("groups", "rows"), "heads", None, None),
            P(("groups", "rows"), "heads", None),
            P(("groups", "rows"), "heads", None),
            P(("groups", "rows")),
            P(),
            P("heads", None),
            P("heads", None),
            P("heads", None),
            P(("rows", "heads"), None),
            P(("rows", "heads"), None),
            P(("rows", "heads"), None),
            P(("groups", "rows"), None),
        ),
        out_specs=P(("groups", "rows"), "heads"),
        check_vma=False,
    )
```

```python
import functools

import jax
import jax.numpy as jnp
from jax import lax
from jax.experimental import pallas as pl
from jax.experimental.pallas import tpu as pltpu
from jax.sharding import PartitionSpec as P

HD = 128
GROUP = 16
CAP = 2
REQ = 8
LANES = 512
F32 = jnp.float32
BF16 = jnp.bfloat16
MESH = pl.DeviceIdType.MESH


def iota(shape, axis):
    return lax.broadcasted_iota(jnp.int32, shape, axis)


def div(v, k):
    return lax.shift_right_logical(v, k.bit_length() - 1) if k & (k - 1) == 0 else lax.div(v, k)


def rem(v, k):
    return v & (k - 1) if k & (k - 1) == 0 else lax.rem(v, k)


def onehot(hit):
    return jnp.where(hit, 1.0, 0.0).astype(BF16)


def dot(a, b):
    return jnp.dot(a, b, preferred_element_type=F32)


def dot_t(a, b):
    return lax.dot_general(a, b, (((1,), (1,)), ((), ())), preferred_element_type=F32)


def loop(count, body):
    if count <= 8:
        for step in range(count):
            body(step)
    else:
        lax.fori_loop(0, count, lambda step, carry: (body(step), carry)[1], 0)


def kernel(n, nb, ctx, nhot, ncold, width, *refs):
    (
        q_hbm, res_hbm, kn_hbm, vn_hbm, gain_hbm, len_hbm, act_hbm,
        kc_hbm, vc_hbm, hg_hbm, hu_hbm, hd_hbm, cg_hbm, cu_hbm, cd_hbm,
        out_ref,
        q_ref, res_ref, kn_ref, vn_ref, gain_ref, len_ref, act_ref,
        sel_v, back_v, turn_v, hid_v,
        kc_v, vc_v, hgu_v, hd_v, cgu_v, cd_v,
        xh, dsp, inc, rout, ret, hot_send, hot_recv, cold_acc,
        load_sem, swap_send, swap_recv, x_sem, hot_sem,
        dsp_sem, inc_sem, rout_sem, ret_sem,
    ) = refs
    half = width // 2
    chunks = half // LANES
    per = n // nb
    row = lax.axis_index("rows")
    h = lax.axis_index("heads")
    other = 1 - h
    t = lax.rem(row, 2)
    idx = lax.div(row, 2)
    partner = {"heads": other}

    barrier = pltpu.get_barrier_semaphore()

    def greet(peer, core):
        pl.semaphore_signal(
            barrier, inc=1, device_id={"rows": peer, "heads": core}, device_id_type=MESH
        )

    loop(n - 1, lambda step: greet(lax.rem(row + step + 1, n), t))
    pl.semaphore_signal(barrier, inc=1, device_id=partner, device_id_type=MESH)

    @pl.when(t == h)
    def _():
        loop(n // 2 - 1, lambda step: greet(lax.rem(row + 2 * step + 2, n), 1 - t))

    @pl.when(t != h)
    def _():
        loop(n // 2, lambda step: greet(lax.rem(row + 2 * step + 1, n), 1 - t))

    loads = [
        (kc_hbm, kc_v),
        (vc_hbm, vc_v),
        (cg_hbm, cgu_v.at[pl.ds(pl.multiple_of(h * ncold, ncold), ncold)]),
        (cu_hbm, cgu_v.at[pl.ds(pl.multiple_of((2 + h) * ncold, ncold), ncold)]),
        (hg_hbm, hgu_v.at[pl.ds(0, nhot)]),
        (hu_hbm, hgu_v.at[pl.ds(nhot, nhot)]),
        (cd_hbm, cd_v.at[pl.ds(pl.multiple_of(h * ncold, ncold), ncold)]),
        (hd_hbm, hd_v),
        (q_hbm, q_ref),
        (kn_hbm, kn_ref),
        (vn_hbm, vn_ref),
        (res_hbm, res_ref),
        (gain_hbm, gain_ref),
        (len_hbm, len_ref),
        (act_hbm, act_ref),
    ]
    loads = [
        pltpu.make_async_copy(src, dst, load_sem.at[i]) for i, (src, dst) in enumerate(loads)
    ]
    for i in (14, 13, 8, 0, 9, 1, 10, 11, 12):
        loads[i].start()

    stack = chunks * REQ
    pay = CAP * chunks
    loads[13].wait()
    loads[14].wait()

    def slots(i):
        targets = []
        for b in range(4):
            count = jnp.int32(0)
            places = [jnp.int32(-1)] * CAP
            for r in range(REQ):
                on = act_ref[i * 4 + b, r]
                for s in range(CAP):
                    places[s] = jnp.where(
                        jnp.logical_and(on == 1, count == s), jnp.int32(r), places[s]
                    )
                count = count + on
            targets += places
        return targets

    def prepare(i):
        line = iota((4 * pay, 1), 0)
        target = jnp.full((4 * pay, 1), -1, jnp.int32)
        for k, p in enumerate(slots(i)):
            target = jnp.where(div(line, chunks) == k, p, target)
        target = jnp.where(target < 0, -1, rem(line, chunks) * REQ + target)
        sel_v[i] = onehot(iota((4 * pay, stack), 1) == target)
    loop(nb // 4, prepare)
    for i in (2, 3, 6, 4, 5, 7):
        loads[i].start()

    scale = 1.0 / HD**0.5
    span = REQ * ctx
    rows_q = GROUP * REQ
    col = iota((1, span + HD), 1)
    whose = jnp.where(jnp.logical_and(col >= span, col < span + REQ), col - span, -1)
    for r in range(REQ):
        here = jnp.logical_and(col >= r * ctx, col < r * ctx + len_ref[r])
        whose = jnp.where(here, r, whose)
    mask = rem(iota((rows_q, span + HD), 0), REQ) == whose
    blank = jnp.zeros((HD - REQ, HD), F32)
    ones = jnp.ones((span + HD, HD), BF16)
    for i in (8, 0, 9, 1, 10, 11):
        loads[i].wait()

    q = q_ref[...].astype(F32)
    kv_local = kc_v.shape[1]
    tiles = []

    def attend(g):
        qs = jnp.concatenate(
            [q[:, (g * GROUP + j) * HD:(g * GROUP + j + 1) * HD] for j in range(GROUP)], axis=0
        )
        key_own = jnp.concatenate([kn_ref[:, g, :].astype(F32), blank], axis=0).astype(BF16)
        keys = jnp.concatenate([kc_v[:, g].reshape(span, HD), key_own], axis=0)
        s = jnp.where(mask, dot_t(qs.astype(BF16), keys) * scale, -1e30)
        e = jnp.exp(s - jnp.max(s, axis=-1, keepdims=True))
        value_own = jnp.concatenate([vn_ref[:, g, :].astype(F32), blank], axis=0).astype(BF16)
        values = jnp.concatenate([vc_v[:, g].reshape(span, HD), value_own], axis=0)
        o = dot(e.astype(BF16), jnp.concatenate([values, ones], axis=1))
        o = o[:, :HD] / o[:, HD:]
        for j in range(GROUP):
            tiles.append(o[j * REQ:(j + 1) * REQ])

    for g in range(kv_local):
        attend(g)

    per_chunk = LANES // HD
    residual = res_ref[...].astype(F32)
    x = jnp.concatenate(
        [
            residual[:, c * LANES:(c + 1) * LANES]
            + jnp.concatenate(tiles[c * per_chunk:(c + 1) * per_chunk], axis=1)
            for c in range(chunks)
        ],
        axis=0,
    ).astype(BF16)
    xh[h] = x

    def select(i):
        dsp[pl.ds(i * 4, 4)] = dot(sel_v[i], x).astype(BF16).reshape(4, pay, LANES)

    loop(nb // 4, select)

    pl.semaphore_wait(barrier, n + n // 2 - jnp.where(t == h, 1, 0))

    side = n // 2

    def dispatch(step):
        dst = lax.rem(row + step, n)
        return pltpu.make_async_remote_copy(
            dsp.at[lax.div(dst, per)], inc.at[h * side + idx], dsp_sem, inc_sem,
            device_id={"rows": dst, "heads": t}, device_id_type=MESH,
        )

    loop(n - 1, lambda step: dispatch(step + 1).start())

    @pl.when(t == h)
    def _():
        pltpu.make_async_copy(dsp.at[lax.div(row, per)], inc.at[h * side + idx], inc_sem).start()

    @pl.when(t != h)
    def _():
        dispatch(0).start()

    send_x = pltpu.make_async_remote_copy(
        xh.at[h], xh.at[h], x_sem.at[0], x_sem.at[1], device_id=partner, device_id_type=MESH
    )
    send_x.start()
    swaps = []
    for hbm, held, base in ((cg_hbm, cgu_v, h), (cu_hbm, cgu_v, 2 + h), (cd_hbm, cd_v, h)):
        for line in range(0, ncold, ncold // 2):
            lines = pl.ds(pl.multiple_of(base * ncold + line, ncold // 2), ncold // 2)
            for hf in range(2):
                columns = pl.ds(hf * half, half)
                swaps.append(
                    pltpu.make_async_remote_copy(
                        hbm.at[pl.ds(line, ncold // 2), columns],
                        held.at[lines, columns],
                        swap_send.at[len(swaps)],
                        swap_recv.at[len(swaps)],
                        device_id=partner,
                        device_id_type=MESH,
                    )
                )
    for copy in swaps:
        copy.start()

    def prepare_back(i):
        column = iota((1, 4 * per * pay), 1)
        slot = div(column, pay * per) * CAP + rem(div(column, chunks), CAP)
        target = jnp.full(column.shape, -1, jnp.int32)
        for k, p in enumerate(slots(i)):
            target = jnp.where(slot == k, p, target)
        target = jnp.where(target < 0, -1, rem(column, chunks) * REQ + target)
        back_v[i] = onehot(iota((stack, 4 * per * pay), 0) == target)

    loop(nb // 4, prepare_back)

    def hidden(blocks, weights, count):
        total = blocks[0] * blocks[0]
        for block in blocks[1:]:
            total = total + block * block
        rs = lax.rsqrt(jnp.sum(total, axis=-1, keepdims=True) / width + 1e-05)
        normed = jnp.concatenate(
            [
                (
                    block * gain_ref[c * LANES:(c + 1) * LANES].astype(F32)[None, :]
                ).astype(BF16)
                for c, block in enumerate(blocks)
            ],
            axis=1,
        )
        both = dot_t(normed, weights) * rs
        gate, up = both[:, :count], both[:, count:]
        return (gate / (1.0 + jnp.exp(-gate)) * up).astype(BF16)

    loads[4].wait()
    loads[5].wait()
    loads[12].wait()
    send_x.wait()
    whole = [xh[side].astype(F32) for side in range(2)]
    hot_hidden = hidden(
        [whole[c // chunks][(c % chunks) * REQ:(c % chunks + 1) * REQ] for c in range(2 * chunks)],
        hgu_v[...],
        nhot,
    )

    loads[2].wait()
    loads[3].wait()
    loads[6].wait()
    for copy in swaps:
        copy.wait()

    def arrive(buffer, sem):
        pltpu.make_async_remote_copy(
            buffer, buffer, dsp_sem, sem, device_id=partner, device_id_type=MESH
        ).wait_recv()

    def drain(buffer, sem):
        def leave(part):
            pltpu.make_async_remote_copy(
                part, part, sem, inc_sem, device_id=partner, device_id_type=MESH
            ).wait_send()

        leave(buffer.at[pl.ds(0, n - 1)])

        @pl.when(t != h)
        def _():
            leave(buffer.at[n - 1])

    big = 4 * pay
    arrive(inc, inc_sem)

    def own(i):
        for hf in range(2):
            came = inc[pl.ds(hf * side + i * 4, 4)].reshape(big, LANES).astype(F32)
            for l in range(per_chunk):
                turn_v[hf, l] = came[:, l * HD:(l + 1) * HD]
        hid_v[i] = hidden(
            [
                jnp.concatenate(
                    [
                        turn_v[c // chunks, l, pl.ds(c % chunks, 8, stride=chunks)]
                        for l in range(per_chunk)
                    ],
                    axis=1,
                )
                for c in range(2 * chunks)
            ],
            cgu_v[...],
            2 * ncold,
        )

    loop(n // 8, own)

    def back(i, hf):
        return pltpu.make_async_remote_copy(
            rout.at[hf * side + i], ret.at[row], rout_sem, ret_sem,
            device_id={"rows": 2 * i + h, "heads": hf}, device_id_type=MESH,
        )

    for hf in range(2):
        def down(i):
            o = dot(hid_v[i], cd_v[:, hf * half:(hf + 1) * half])
            for c in range(chunks):
                for l in range(per_chunk):
                    turn_v[hf, l, pl.ds(c, 8, stride=chunks)] = (
                        o[:, c * LANES + l * HD:c * LANES + (l + 1) * HD]
                    )
            turned = jnp.concatenate([turn_v[hf, l] for l in range(per_chunk)], axis=1)
            rout[pl.ds(hf * side + i * 4, 4)] = turned.astype(BF16).reshape(4, pay, LANES)

        loop(n // 8, down)

        def give(step):
            offset = jnp.where(idx < side // 2, side - 1 - step, step + 1)
            back(lax.rem(idx + offset, side), hf).start()

        loop(side - 1, give)
        here = jnp.logical_and(t == h, h == hf)

        @pl.when(here)
        def _():
            pltpu.make_async_copy(rout.at[hf * side + idx], ret.at[row], ret_sem).start()

        @pl.when(jnp.logical_not(here))
        def _():
            back(idx, hf).start()

    loads[7].wait()

    def hot_down(side):
        part = dot(hot_hidden, hd_v[:, pl.ds(pl.multiple_of(side * half, half), half)])
        return jnp.concatenate(
            [part[:, c * LANES:(c + 1) * LANES] for c in range(chunks)], axis=0
        )

    hot_send[...] = hot_down(other)
    send_hot = pltpu.make_async_remote_copy(
        hot_send, hot_recv, hot_sem.at[0], hot_sem.at[1], device_id=partner, device_id_type=MESH
    )
    send_hot.start()
    result = hot_down(h) + x.astype(F32)

    drain(inc, dsp_sem)
    drain(rout, rout_sem)

    cold_acc[...] = result
    arrive(ret, ret_sem)

    def collect(i):
        cold_acc[...] += dot(
            back_v[i], ret[pl.ds(i * 4 * per, 4 * per)].reshape(4 * per * pay, LANES)
        )

    loop(nb // 4, collect)
    send_hot.wait()
    result = cold_acc[...] + hot_recv[...]
    for c in range(chunks):
        out_ref[:, c * LANES:(c + 1) * LANES] = result[c * REQ:(c + 1) * REQ].astype(out_ref.dtype)


def local(n, residual_in, query, key_cache, value_cache, key_new, value_new, lengths, norm_gain,
          hot_gate, hot_up, hot_down, cold_gate, cold_up, cold_down, active):
    width = hot_gate.shape[1]
    half = width // 2
    chunks = half // LANES
    nb = active.shape[1]
    nhot, ncold = hot_gate.shape[0], cold_gate.shape[0]
    ctx = key_cache.shape[2]
    vmem = pl.BlockSpec(memory_space=pltpu.VMEM)
    hbm = pl.BlockSpec(memory_space=pltpu.HBM)
    pay = CAP * chunks
    dma = pltpu.SemaphoreType.DMA
    return pl.pallas_call(
        functools.partial(kernel, n, nb, ctx, nhot, ncold, width),
        out_shape=pltpu.VMEM(residual_in.shape, residual_in.dtype),
        in_specs=[hbm] * 15,
        out_specs=vmem,
        scratch_shapes=[
            pltpu.VMEM(query.shape, BF16),
            pltpu.VMEM(residual_in.shape, BF16),
            pltpu.VMEM(key_new.shape, BF16),
            pltpu.VMEM(value_new.shape, BF16),
            pltpu.VMEM(norm_gain.shape, BF16),
            pltpu.SMEM(lengths.shape, jnp.int32),
            pltpu.SMEM(active.shape[::-1], jnp.int32),
            pltpu.VMEM((nb // 4, 4 * pay, chunks * REQ), BF16),
            pltpu.VMEM((nb // 4, chunks * REQ, 4 * (n // nb) * pay), BF16),
            pltpu.VMEM((2, LANES // HD, 4 * pay, HD), F32),
            pltpu.VMEM((n // 8, 8, 2 * ncold), BF16),
            pltpu.VMEM(key_cache.shape, BF16),
            pltpu.VMEM(value_cache.shape, BF16),
            pltpu.VMEM((2 * nhot, width), BF16),
            pltpu.VMEM((nhot, width), BF16),
            pltpu.VMEM((4 * ncold, width), BF16),
            pltpu.VMEM((2 * ncold, width), BF16),
            pltpu.VMEM((2, chunks * REQ, LANES), BF16),
            pltpu.VMEM((nb, pay, LANES), BF16),
            pltpu.VMEM((n, pay, LANES), BF16),
            pltpu.VMEM((n, pay, LANES), BF16),
            pltpu.VMEM((n, pay, LANES), BF16),
            pltpu.VMEM((chunks * REQ, LANES), F32),
            pltpu.VMEM((chunks * REQ, LANES), F32),
            pltpu.VMEM((chunks * REQ, LANES), F32),
            dma((15,)), dma((12,)), dma((12,)), dma((2,)), dma((2,)),
            dma(()), dma(()), dma(()), dma(()),
        ],
        compiler_params=pltpu.CompilerParams(
            collective_id=0, has_side_effects=True, vmem_limit_bytes=48 * 1024 * 1024
        ),
        name="decode_step",
    )(*[
        pltpu.with_memory_space_constraint(array, pltpu.HBM)
        for array in (
            query, residual_in, key_new, value_new, norm_gain, lengths, active.T,
            key_cache, value_cache, hot_gate, hot_up, hot_down, cold_gate, cold_up, cold_down,
        )
    ])


def solution(mesh):
    return jax.shard_map(
        functools.partial(local, mesh.shape["rows"]),
        mesh=mesh,
        in_specs=(
            P(("groups", "rows"), "heads"),
            P(("groups", "rows"), "heads"),
            P(("groups", "rows"), "heads", None, None),
            P(("groups", "rows"), "heads", None, None),
            P(("groups", "rows"), "heads", None),
            P(("groups", "rows"), "heads", None),
            P(("groups", "rows")),
            P(),
            P("heads", None),
            P("heads", None),
            P("heads", None),
            P(("rows", "heads"), None),
            P(("rows", "heads"), None),
            P(("rows", "heads"), None),
            P(("groups", "rows"), None),
        ),
        out_specs=P(("groups", "rows"), "heads"),
        check_vma=False,
    )
```

```python
import functools

import jax
import jax.numpy as jnp
from jax import lax
from jax.experimental import pallas as pl
from jax.experimental.pallas import tpu as pltpu
from jax.sharding import PartitionSpec as P

HD = 128
GROUP = 16
CAP = 2
REQ = 8
LANES = 512
F32 = jnp.float32
BF16 = jnp.bfloat16
MESH = pl.DeviceIdType.MESH


def iota(shape, axis):
    return lax.broadcasted_iota(jnp.int32, shape, axis)


def div(v, k):
    return lax.shift_right_logical(v, k.bit_length() - 1) if k & (k - 1) == 0 else lax.div(v, k)


def rem(v, k):
    return v & (k - 1) if k & (k - 1) == 0 else lax.rem(v, k)


def onehot(hit):
    return jnp.where(hit, 1.0, 0.0).astype(BF16)


def dot(a, b):
    return jnp.dot(a, b, preferred_element_type=F32)


def dot_t(a, b):
    return lax.dot_general(a, b, (((1,), (1,)), ((), ())), preferred_element_type=F32)


def loop(count, body):
    if count <= 8:
        for step in range(count):
            body(step)
    else:
        lax.fori_loop(0, count, lambda step, carry: (body(step), carry)[1], 0)


def kernel(n, nb, ctx, nhot, ncold, width, *refs):
    (
        q_hbm, res_hbm, kn_hbm, vn_hbm, gain_hbm, len_hbm, act_hbm,
        kc_hbm, vc_hbm, hg_hbm, hu_hbm, hd_hbm, cg_hbm, cu_hbm, cd_hbm,
        out_ref,
        q_ref, res_ref, kn_ref, vn_ref, gain_ref, len_ref, act_ref,
        sel_v, back_v, turn_v, hid_v,
        kc_v, vc_v, hgu_v, hd_v, cgu_v, cd_v,
        xh, dsp, inc, rout, ret, hot_send, hot_recv, cold_acc,
        load_sem, swap_send, swap_recv, x_sem, hot_sem,
        dsp_sem, inc_sem, rout_sem, ret_sem,
    ) = refs
    half = width // 2
    chunks = half // LANES
    per = n // nb
    row = lax.axis_index("rows")
    h = lax.axis_index("heads")
    other = 1 - h
    t = lax.rem(row, 2)
    idx = lax.div(row, 2)
    partner = {"heads": other}

    barrier = pltpu.get_barrier_semaphore()

    def greet(peer, core):
        pl.semaphore_signal(
            barrier, inc=1, device_id={"rows": peer, "heads": core}, device_id_type=MESH
        )

    loop(n - 1, lambda step: greet(lax.rem(row + step + 1, n), t))
    pl.semaphore_signal(barrier, inc=1, device_id=partner, device_id_type=MESH)

    @pl.when(t == h)
    def _():
        loop(n // 2 - 1, lambda step: greet(lax.rem(row + 2 * step + 2, n), 1 - t))

    @pl.when(t != h)
    def _():
        loop(n // 2, lambda step: greet(lax.rem(row + 2 * step + 1, n), 1 - t))

    loads = [
        (kc_hbm, kc_v),
        (vc_hbm, vc_v),
        (cg_hbm, cgu_v.at[pl.ds(pl.multiple_of(h * ncold, ncold), ncold)]),
        (cu_hbm, cgu_v.at[pl.ds(pl.multiple_of((2 + h) * ncold, ncold), ncold)]),
        (hg_hbm, hgu_v.at[pl.ds(0, nhot)]),
        (hu_hbm, hgu_v.at[pl.ds(nhot, nhot)]),
        (cd_hbm, cd_v.at[pl.ds(pl.multiple_of(h * ncold, ncold), ncold)]),
        (hd_hbm, hd_v),
        (q_hbm, q_ref),
        (kn_hbm, kn_ref),
        (vn_hbm, vn_ref),
        (res_hbm, res_ref),
        (gain_hbm, gain_ref),
        (len_hbm, len_ref),
        (act_hbm, act_ref),
    ]
    loads = [
        pltpu.make_async_copy(src, dst, load_sem.at[i]) for i, (src, dst) in enumerate(loads)
    ]
    for i in (14, 13, 8, 0, 9, 1, 10, 11, 12):
        loads[i].start()

    stack = chunks * REQ
    pay = CAP * chunks
    loads[13].wait()
    loads[14].wait()

    def slots(i):
        targets = []
        for b in range(4):
            count = jnp.int32(0)
            places = [jnp.int32(-1)] * CAP
            for r in range(REQ):
                on = act_ref[i * 4 + b, r]
                for s in range(CAP):
                    places[s] = jnp.where(
                        jnp.logical_and(on == 1, count == s), jnp.int32(r), places[s]
                    )
                count = count + on
            targets += places
        return targets

    def prepare(i):
        line = iota((4 * pay, 1), 0)
        target = jnp.full((4 * pay, 1), -1, jnp.int32)
        for k, p in enumerate(slots(i)):
            target = jnp.where(div(line, chunks) == k, p, target)
        target = jnp.where(target < 0, -1, rem(line, chunks) * REQ + target)
        sel_v[i] = onehot(iota((4 * pay, stack), 1) == target)
    loop(nb // 4, prepare)
    for i in (2, 3, 6, 4, 5, 7):
        loads[i].start()

    scale = 1.0 / HD**0.5
    span = REQ * ctx
    rows_q = GROUP * REQ
    col = iota((1, span + HD), 1)
    whose = jnp.where(jnp.logical_and(col >= span, col < span + REQ), col - span, -1)
    for r in range(REQ):
        here = jnp.logical_and(col >= r * ctx, col < r * ctx + len_ref[r])
        whose = jnp.where(here, r, whose)
    mask = rem(iota((rows_q, span + HD), 0), REQ) == whose
    blank = jnp.zeros((HD - REQ, HD), F32)
    ones = jnp.ones((span + HD, HD), BF16)
    for i in (8, 0, 9, 1, 10, 11):
        loads[i].wait()

    q = q_ref[...].astype(F32)
    kv_local = kc_v.shape[1]
    tiles = []

    def attend(g):
        qs = jnp.concatenate(
            [q[:, (g * GROUP + j) * HD:(g * GROUP + j + 1) * HD] for j in range(GROUP)], axis=0
        )
        key_own = jnp.concatenate([kn_ref[:, g, :].astype(F32), blank], axis=0).astype(BF16)
        keys = jnp.concatenate([kc_v[:, g].reshape(span, HD), key_own], axis=0)
        s = jnp.where(mask, dot_t(qs.astype(BF16), keys) * scale, -1e30)
        e = jnp.exp(s - jnp.max(s, axis=-1, keepdims=True))
        value_own = jnp.concatenate([vn_ref[:, g, :].astype(F32), blank], axis=0).astype(BF16)
        values = jnp.concatenate([vc_v[:, g].reshape(span, HD), value_own], axis=0)
        o = dot(e.astype(BF16), jnp.concatenate([values, ones], axis=1))
        o = o[:, :HD] / o[:, HD:]
        for j in range(GROUP):
            tiles.append(o[j * REQ:(j + 1) * REQ])

    for g in range(kv_local):
        attend(g)

    per_chunk = LANES // HD
    residual = res_ref[...].astype(F32)
    x = jnp.concatenate(
        [
            residual[:, c * LANES:(c + 1) * LANES]
            + jnp.concatenate(tiles[c * per_chunk:(c + 1) * per_chunk], axis=1)
            for c in range(chunks)
        ],
        axis=0,
    ).astype(BF16)
    xh[h] = x

    def select(i):
        dsp[pl.ds(i * 4, 4)] = dot(sel_v[i], x).astype(BF16).reshape(4, pay, LANES)

    loop(nb // 4, select)

    pl.semaphore_wait(barrier, n + n // 2 - jnp.where(t == h, 1, 0))

    side = n // 2

    def dispatch(step):
        dst = lax.rem(row + step, n)
        return pltpu.make_async_remote_copy(
            dsp.at[lax.div(dst, per)], inc.at[h * side + idx], dsp_sem, inc_sem,
            device_id={"rows": dst, "heads": t}, device_id_type=MESH,
        )

    loop(n - 1, lambda step: dispatch(step + 1).start())

    @pl.when(t == h)
    def _():
        pltpu.make_async_copy(dsp.at[lax.div(row, per)], inc.at[h * side + idx], inc_sem).start()

    @pl.when(t != h)
    def _():
        dispatch(0).start()

    send_x = pltpu.make_async_remote_copy(
        xh.at[h], xh.at[h], x_sem.at[0], x_sem.at[1], device_id=partner, device_id_type=MESH
    )
    send_x.start()
    swaps = [
        (cg_hbm, cgu_v.at[pl.ds(pl.multiple_of(h * ncold, ncold), ncold)]),
        (cu_hbm, cgu_v.at[pl.ds(pl.multiple_of((2 + h) * ncold, ncold), ncold)]),
        (cd_hbm, cd_v.at[pl.ds(pl.multiple_of(h * ncold, ncold), ncold)]),
    ]
    swaps = [
        pltpu.make_async_remote_copy(
            src, dst, swap_send.at[i], swap_recv.at[i], device_id=partner, device_id_type=MESH
        )
        for i, (src, dst) in enumerate(swaps)
    ]
    for copy in swaps:
        copy.start()

    def prepare_back(i):
        column = iota((1, 4 * per * pay), 1)
        slot = div(column, pay * per) * CAP + rem(div(column, chunks), CAP)
        target = jnp.full(column.shape, -1, jnp.int32)
        for k, p in enumerate(slots(i)):
            target = jnp.where(slot == k, p, target)
        target = jnp.where(target < 0, -1, rem(column, chunks) * REQ + target)
        back_v[i] = onehot(iota((stack, 4 * per * pay), 0) == target)

    loop(nb // 4, prepare_back)

    def hidden(blocks, weights, count):
        total = blocks[0] * blocks[0]
        for block in blocks[1:]:
            total = total + block * block
        rs = lax.rsqrt(jnp.sum(total, axis=-1, keepdims=True) / width + 1e-05)
        normed = jnp.concatenate(
            [
                (
                    block * gain_ref[c * LANES:(c + 1) * LANES].astype(F32)[None, :]
                ).astype(BF16)
                for c, block in enumerate(blocks)
            ],
            axis=1,
        )
        both = dot_t(normed, weights) * rs
        gate, up = both[:, :count], both[:, count:]
        return (gate / (1.0 + jnp.exp(-gate)) * up).astype(BF16)

    loads[12].wait()
    loads[2].wait()
    loads[3].wait()
    loads[6].wait()
    for copy in swaps:
        copy.wait()

    def arrive(buffer, sem):
        pltpu.make_async_remote_copy(
            buffer, buffer, dsp_sem, sem, device_id=partner, device_id_type=MESH
        ).wait_recv()

    def drain(buffer, sem):
        def leave(part):
            pltpu.make_async_remote_copy(
                part, part, sem, inc_sem, device_id=partner, device_id_type=MESH
            ).wait_send()

        leave(buffer.at[pl.ds(0, n - 1)])

        @pl.when(t != h)
        def _():
            leave(buffer.at[n - 1])

    big = 4 * pay
    arrive(inc, inc_sem)

    def own(i):
        for hf in range(2):
            came = inc[pl.ds(hf * side + i * 4, 4)].reshape(big, LANES).astype(F32)
            for l in range(per_chunk):
                turn_v[hf, l] = came[:, l * HD:(l + 1) * HD]
        hid_v[i] = hidden(
            [
                jnp.concatenate(
                    [
                        turn_v[c // chunks, l, pl.ds(c % chunks, 8, stride=chunks)]
                        for l in range(per_chunk)
                    ],
                    axis=1,
                )
                for c in range(2 * chunks)
            ],
            cgu_v[...],
            2 * ncold,
        )

    loop(n // 8, own)

    def back(i, hf):
        return pltpu.make_async_remote_copy(
            rout.at[hf * side + i], ret.at[row], rout_sem, ret_sem,
            device_id={"rows": 2 * i + h, "heads": hf}, device_id_type=MESH,
        )

    for hf in range(2):
        def down(i):
            o = dot(hid_v[i], cd_v[:, hf * half:(hf + 1) * half])
            for c in range(chunks):
                for l in range(per_chunk):
                    turn_v[hf, l, pl.ds(c, 8, stride=chunks)] = (
                        o[:, c * LANES + l * HD:c * LANES + (l + 1) * HD]
                    )
            turned = jnp.concatenate([turn_v[hf, l] for l in range(per_chunk)], axis=1)
            rout[pl.ds(hf * side + i * 4, 4)] = turned.astype(BF16).reshape(4, pay, LANES)

        loop(n // 8, down)

        def give(step):
            offset = jnp.where(idx < side // 2, side - 1 - step, step + 1)
            back(lax.rem(idx + offset, side), hf).start()

        loop(side - 1, give)
        here = jnp.logical_and(t == h, h == hf)

        @pl.when(here)
        def _():
            pltpu.make_async_copy(rout.at[hf * side + idx], ret.at[row], ret_sem).start()

        @pl.when(jnp.logical_not(here))
        def _():
            back(idx, hf).start()

    loads[4].wait()
    loads[5].wait()
    send_x.wait()
    whole = [xh[side].astype(F32) for side in range(2)]
    hot_hidden = hidden(
        [whole[c // chunks][(c % chunks) * REQ:(c % chunks + 1) * REQ] for c in range(2 * chunks)],
        hgu_v[...],
        nhot,
    )

    loads[7].wait()

    def hot_down(side):
        part = dot(hot_hidden, hd_v[:, pl.ds(pl.multiple_of(side * half, half), half)])
        return jnp.concatenate(
            [part[:, c * LANES:(c + 1) * LANES] for c in range(chunks)], axis=0
        )

    hot_send[...] = hot_down(other)
    send_hot = pltpu.make_async_remote_copy(
        hot_send, hot_recv, hot_sem.at[0], hot_sem.at[1], device_id=partner, device_id_type=MESH
    )
    send_hot.start()
    result = hot_down(h) + x.astype(F32)

    drain(inc, dsp_sem)
    drain(rout, rout_sem)

    cold_acc[...] = result
    arrive(ret, ret_sem)

    def collect(i):
        cold_acc[...] += dot(
            back_v[i], ret[pl.ds(i * 4 * per, 4 * per)].reshape(4 * per * pay, LANES)
        )

    loop(nb // 4, collect)
    send_hot.wait()
    result = cold_acc[...] + hot_recv[...]
    for c in range(chunks):
        out_ref[:, c * LANES:(c + 1) * LANES] = result[c * REQ:(c + 1) * REQ].astype(out_ref.dtype)


def local(n, residual_in, query, key_cache, value_cache, key_new, value_new, lengths, norm_gain,
          hot_gate, hot_up, hot_down, cold_gate, cold_up, cold_down, active):
    width = hot_gate.shape[1]
    half = width // 2
    chunks = half // LANES
    nb = active.shape[1]
    nhot, ncold = hot_gate.shape[0], cold_gate.shape[0]
    ctx = key_cache.shape[2]
    vmem = pl.BlockSpec(memory_space=pltpu.VMEM)
    hbm = pl.BlockSpec(memory_space=pltpu.HBM)
    pay = CAP * chunks
    dma = pltpu.SemaphoreType.DMA
    return pl.pallas_call(
        functools.partial(kernel, n, nb, ctx, nhot, ncold, width),
        out_shape=pltpu.VMEM(residual_in.shape, residual_in.dtype),
        in_specs=[hbm] * 15,
        out_specs=vmem,
        scratch_shapes=[
            pltpu.VMEM(query.shape, BF16),
            pltpu.VMEM(residual_in.shape, BF16),
            pltpu.VMEM(key_new.shape, BF16),
            pltpu.VMEM(value_new.shape, BF16),
            pltpu.VMEM(norm_gain.shape, BF16),
            pltpu.SMEM(lengths.shape, jnp.int32),
            pltpu.SMEM(active.shape[::-1], jnp.int32),
            pltpu.VMEM((nb // 4, 4 * pay, chunks * REQ), BF16),
            pltpu.VMEM((nb // 4, chunks * REQ, 4 * (n // nb) * pay), BF16),
            pltpu.VMEM((2, LANES // HD, 4 * pay, HD), F32),
            pltpu.VMEM((n // 8, 8, 2 * ncold), BF16),
            pltpu.VMEM(key_cache.shape, BF16),
            pltpu.VMEM(value_cache.shape, BF16),
            pltpu.VMEM((2 * nhot, width), BF16),
            pltpu.VMEM((nhot, width), BF16),
            pltpu.VMEM((4 * ncold, width), BF16),
            pltpu.VMEM((2 * ncold, width), BF16),
            pltpu.VMEM((2, chunks * REQ, LANES), BF16),
            pltpu.VMEM((nb, pay, LANES), BF16),
            pltpu.VMEM((n, pay, LANES), BF16),
            pltpu.VMEM((n, pay, LANES), BF16),
            pltpu.VMEM((n, pay, LANES), BF16),
            pltpu.VMEM((chunks * REQ, LANES), F32),
            pltpu.VMEM((chunks * REQ, LANES), F32),
            pltpu.VMEM((chunks * REQ, LANES), F32),
            dma((15,)), dma((3,)), dma((3,)), dma((2,)), dma((2,)),
            dma(()), dma(()), dma(()), dma(()),
        ],
        compiler_params=pltpu.CompilerParams(
            collective_id=0, has_side_effects=True, vmem_limit_bytes=48 * 1024 * 1024
        ),
        name="decode_step",
    )(*[
        pltpu.with_memory_space_constraint(array, pltpu.HBM)
        for array in (
            query, residual_in, key_new, value_new, norm_gain, lengths, active.T,
            key_cache, value_cache, hot_gate, hot_up, hot_down, cold_gate, cold_up, cold_down,
        )
    ])


def solution(mesh):
    return jax.shard_map(
        functools.partial(local, mesh.shape["rows"]),
        mesh=mesh,
        in_specs=(
            P(("groups", "rows"), "heads"),
            P(("groups", "rows"), "heads"),
            P(("groups", "rows"), "heads", None, None),
            P(("groups", "rows"), "heads", None, None),
            P(("groups", "rows"), "heads", None),
            P(("groups", "rows"), "heads", None),
            P(("groups", "rows")),
            P(),
            P("heads", None),
            P("heads", None),
            P("heads", None),
            P(("rows", "heads"), None),
            P(("rows", "heads"), None),
            P(("rows", "heads"), None),
            P(("groups", "rows"), None),
        ),
        out_specs=P(("groups", "rows"), "heads"),
        check_vma=False,
    )
```
